768 devices in a mesh: fsdp: 96 (over y, z_hi, x), tp: 8 (over z_lo, core).
Axes of the slice: x: 4, y: 8, z: 12 (z_hi: 3, z_lo: 4; z = z_hi * 4 + z_lo), core: 2. Of those that a mesh axis runs over, the one named last changes fastest.
Arguments:
- tokens: bfloat16 [288, 8192], P('fsdp', 'tp'), may hold values from -6 to 6
- grad_out: bfloat16 [288, 8192], P('fsdp', 'tp'), may hold values from -6 to 6
- gate_codes: bfloat16 [8192, 36864], P('tp', 'fsdp'), may hold values from -0.0625 to 0.0625
- gate_scale: float32 [64, 288], P('tp', 'fsdp'), may hold values from 0.25 to 4
- up_codes: bfloat16 [8192, 36864], P('tp', 'fsdp'), may hold values from -0.0625 to 0.0625
- up_scale: float32 [64, 288], P('tp', 'fsdp'), may hold values from 0.25 to 4
- down_codes: bfloat16 [36864, 8192], P('fsdp', 'tp'), may hold values from -0.03125 to 0.03125
- down_scale: float32 [288, 64], P('fsdp', 'tp'), may hold values from 0.25 to 4
Outputs:
- grad_tokens: bfloat16 [288, 8192], P('fsdp', 'tp')
- grad_gate: bfloat16 [8192, 36864], P('tp', 'fsdp')
- grad_up: bfloat16 [8192, 36864], P('tp', 'fsdp')
- grad_down: bfloat16 [36864, 8192], P('fsdp', 'tp')
The draws below stay inside these ranges and needn't reach their ends.
All inputs are finite; a program needn't handle non-finite values.
Results may differ from the reference program's by a relative error of at most 0.0072.
Values may be sent and summed in bfloat16 or wider, within the bound.
A program may use at most 32 MiB of HBM per device.

```python
import math
import jax
import jax.numpy as jnp
from jax import lax

D = 8192
FF = 36864
TILE = 128
TOKENS = 288


def block_scale(rng, extent, pieces, smallest, top_value):
    factor_of, own = 1.0, jax.random.fold_in(rng, 6)
    for position, shards_of in pieces:
        steps = jnp.exp(jax.random.uniform(jax.random.fold_in(own, position), (shards_of,), jnp.float32, smallest / len(pieces), top_value / len(pieces)))
        factor_of = factor_of * jnp.repeat(steps, extent[position] // shards_of).reshape([-1 if axis == position else 1 for axis in range(len(extent))])
    return factor_of


def noise(stream_key, dims, deviation, bound, split=(), held_as=jnp.bfloat16):
    gain = block_scale(stream_key, dims, split, -0.22, 0.18) if split else 1.0
    values = jax.random.normal(stream_key, dims, jnp.float32) * deviation * gain
    return jnp.minimum(jnp.maximum(values, -bound), bound).astype(held_as)


def setup_inputs(seed: int = 0) -> dict:
    key_of = jax.random.split(jax.random.key(seed), 9)
    return {
        "tokens": noise(key_of[0], (TOKENS, D), 1.0, 6.0, ((0, 96), (1, 8))),
        "grad_out": noise(key_of[1], (TOKENS, D), 1.0, 6.0, ((0, 96), (1, 8))),
        "gate_codes": noise(key_of[2], (D, FF), D ** -0.5, 0.0625, ((0, 8), (1, 96))),
        "gate_scale": jnp.clip(jnp.exp(math.log(4.0) - 2.7725887 * jax.random.uniform(key_of[3], (D // TILE, FF // TILE), jnp.float32) ** block_scale(key_of[3], (D // TILE, FF // TILE), ((0, 8), (1, 96)), -0.2, 0.2)), 0.25, 4.0),
        "up_codes": noise(key_of[4], (D, FF), D ** -0.5, 0.0625, ((0, 8), (1, 96))),
        "up_scale": jnp.clip(jnp.exp(math.log(4.0) - 2.7725887 * jax.random.uniform(key_of[5], (D // TILE, FF // TILE), jnp.float32) ** block_scale(key_of[5], (D // TILE, FF // TILE), ((0, 8), (1, 96)), -0.2, 0.2)), 0.25, 4.0),
        "down_codes": noise(key_of[6], (FF, D), FF ** -0.5, 0.03125, ((0, 96), (1, 8))),
        "down_scale": jnp.clip(jnp.exp(math.log(4.0) - 2.7725887 * jax.random.uniform(key_of[7], (FF // TILE, D // TILE), jnp.float32) ** block_scale(key_of[7], (FF // TILE, D // TILE), ((0, 96), (1, 8)), -0.2, 0.2)), 0.25, 4.0),
    }


def dequantize(codes, scales):
    blocks_down, blocks_across = scales.shape
    tile_rows = codes.shape[0] // blocks_down
    tile_cols = codes.shape[1] // blocks_across
    scaled = codes.astype(jnp.float32).reshape(blocks_down, tile_rows, blocks_across, tile_cols) * scales[:, None, :, None]
    return scaled.reshape(codes.shape).astype(jnp.bfloat16)


def contract(left, right, left_dim, right_dim):
    return lax.dot_general(left, right, (((left_dim,), (right_dim,)), ((), ())), preferred_element_type=jnp.float32)


def reference(tokens, grad_out, gate_codes, gate_scale, up_codes, up_scale, down_codes, down_scale):
    gate_weight = dequantize(gate_codes, gate_scale)
    up_weight = dequantize(up_codes, up_scale)
    down_weight = dequantize(down_codes, down_scale)
    gate = jnp.dot(tokens, gate_weight, preferred_element_type=jnp.float32)
    up_value = jnp.dot(tokens, up_weight, preferred_element_type=jnp.float32)
    grad_hidden = contract(grad_out, down_weight, 1, 1)
    sigma = jax.nn.sigmoid(gate)
    active = gate * sigma
    hidden = (active * up_value).astype(jnp.bfloat16)
    grad_up_pre = (grad_hidden * active).astype(jnp.bfloat16)
    grad_gate_pre = (grad_hidden * up_value * sigma * (1.0 + gate * (1.0 - sigma))).astype(jnp.bfloat16)
    grad_tokens = (contract(grad_gate_pre, gate_weight, 1, 1) + contract(grad_up_pre, up_weight, 1, 1)).astype(jnp.bfloat16)
    grad_gate = contract(tokens, grad_gate_pre, 0, 0).astype(jnp.bfloat16)
    grad_up = contract(tokens, grad_up_pre, 0, 0).astype(jnp.bfloat16)
    grad_down = contract(hidden, grad_out, 0, 0).astype(jnp.bfloat16)
    return (grad_tokens, grad_gate, grad_up, grad_down)
```

```python
import functools

import jax
import jax.numpy as jnp
from jax import lax
from jax.experimental import pallas as pl
from jax.experimental.pallas import tpu as pltpu
from jax.sharding import PartitionSpec as P

BF = jnp.bfloat16
F32 = jnp.float32
NY, NX, NZH, NZ = 8, 4, 3, 4
TOK, FEAT, HID = 288, 1024, 384
SEG = 112
HALF = NZ * SEG
MESH = pl.DeviceIdType.MESH

_IDS = {}


def _id(*key):
    return _IDS.setdefault(key, len(_IDS))


for _a in range(2):
    for _d in (1, 2):
        _id("gz", _a, _d)
    for _d in range(1, NY):
        _id("gy", _a, _d)
    for _k in ("gxr", "gxl", "gxr2", "gxl2"):
        _id(_k, _a)
for _k in range(3):
    _id("core", _k)
    for _d in range(1, NZ):
        _id("z", _k, _d)
for _k in range(2):
    for _d in range(NZ):
        _id("back", _k, _d)
        _id("backcore", _k, _d)
for _k in ("x2r", "x2l", "x1r", "x1l", "xcr", "xcl"):
    _id(_k)
for _d in range(1, NY):
    _id("sy", _d)
for _d in (1, 2):
    _id("sz", _d)
N_IDS = len(_IDS)


def nt(left, right):
    return lax.dot_general(left, right, (((1,), (1,)), ((), ())), preferred_element_type=F32)


def tn(left, right):
    return lax.dot_general(left, right, (((0,), (0,)), ((), ())), preferred_element_type=F32)


def kernel(
    tok, gout, gc, gs, uc, us, dc, dsc,
    gt, gg, gu, gd,
    wg, wu, wd, G, st, X, U, RA, S, RB, HH, T, TB, RX1, RX2, RXa, RXb, CA, CB,
    YB, YF, RY, ZB, RZ, og, ou, od, fin,
    lsem, ssem, rsem,
):
    f = lax.axis_index("fsdp")
    tp = lax.axis_index("tp")
    y, zh, x = f // 12, lax.rem(f // 4, 3), lax.rem(f, 4)
    z, core = tp // 2, lax.rem(tp, 2)

    def dev(y=y, zh=zh, x=x, z=z, core=core):
        return ((y * 3 + zh) * 4 + x, z * 2 + core)

    def wrap(v, n):
        return lax.rem(v + n, n)

    def up(v, d, n):
        return lax.rem(v + d, n)

    def rcopy(key, src, dst, to):
        i = _IDS[key]
        return pltpu.make_async_remote_copy(
            src_ref=src, dst_ref=dst, send_sem=ssem.at[i], recv_sem=rsem.at[i],
            device_id=to, device_id_type=MESH,
        )

    sent = []

    def send(key, src, dst, to):
        c = rcopy(key, src, dst, to)
        c.start()
        sent.append(c)

    def recv(key, dst):
        rcopy(key, dst, dst, dev(core=1 - core)).wait_recv()

    loads = [
        pltpu.make_async_copy(s, d, lsem.at[i])
        for i, (s, d) in enumerate(((gc, wg), (uc, wu), (dc, wd)))
    ]
    for c in loads:
        c.start()

    barrier = pltpu.get_barrier_semaphore()
    partners = (
        [dev(zh=up(zh, d, 3)) for d in (1, 2)]
        + [dev(y=up(y, d, NY)) for d in range(1, NY)]
        + [dev(x=up(x, d, NX)) for d in (1, 3)]
        + [dev(z=up(z, d, NZ)) for d in range(1, NZ)]
        + [dev(core=1 - core)]
    )
    for p in partners:
        pl.semaphore_signal(barrier, inc=1, device_id=p, device_id_type=MESH)

    for a, ref in ((0, tok), (1, gout)):
        v = ref[...].astype(F32)
        for r in range(3):
            for c in range(8):
                st[a * 24 + r * 8 + c : a * 24 + r * 8 + c + 1, :] = v[r : r + 1, c * 128 : (c + 1) * 128]
        G[a, y, x, zh] = st[a * 24 : (a + 1) * 24, :].astype(BF)

    pl.semaphore_wait(barrier, len(partners))

    for a in range(2):
        for d in (1, 2):
            blk = G.at[a, y, x, zh]
            send(("gz", a, d), blk, blk, dev(zh=up(zh, d, 3)))

    def dequant(i, w, sc):
        loads[i].wait()
        nr, nc = w.shape[0] // 128, w.shape[1] // 128
        for r in range(nr):
            for c in range(nc):
                t = w[r * 128 : (r + 1) * 128, c * 128 : (c + 1) * 128]
                w[r * 128 : (r + 1) * 128, c * 128 : (c + 1) * 128] = (t.astype(F32) * sc[r, c]).astype(BF)

    dequant(0, wg, gs)
    for a in range(2):
        for d in (1, 2):
            recv(("gz", a, d), G.at[a, y, x, wrap(zh - d, 3)])
        for d in range(1, NY):
            send(("gy", a, d), G.at[a, y, x], G.at[a, y, x], dev(y=up(y, d, NY)))
    dequant(1, wu, us)
    dequant(2, wd, dsc)
    right, left = dev(x=up(x, 1, NX)), dev(x=up(x, 3, NX))
    xr, xl, xo = up(x, 1, NX), up(x, 3, NX), up(x, 2, NX)
    for a in range(2):
        for d in range(1, NY):
            recv(("gy", a, d), G.at[a, wrap(y - d, NY), x])
        send(("gxr", a), G.at[a, :, x], G.at[a, :, x], right)
        send(("gxl", a), G.at[a, :, x], G.at[a, :, x], left)

    def forward(a):
        recv(("gxr", a), G.at[a, :, xl])
        send(("gxr2", a), G.at[a, 0:4, xl], G.at[a, 0:4, xl], right)
        recv(("gxl", a), G.at[a, :, xr])
        send(("gxl2", a), G.at[a, 4:8, xr], G.at[a, 4:8, xr], left)

    def unpack(a):
        recv(("gxr2", a), G.at[a, 0:4, xo])
        recv(("gxl2", a), G.at[a, 4:8, xo])

        @pl.loop(0, NY)
        def _(yy):
            for xx in range(NX):
                for zz in range(NZH):
                    row = pl.multiple_of((yy * 12 + xx * 3 + zz) * 24, 8)
                    st[pl.ds(row, 24), :] = G[a, yy, xx, zz].astype(F32)

        for c in range(8):
            X[a, :, c * 128 : (c + 1) * 128] = st[pl.ds(c, TOK, stride=8), :].astype(BF)

    other = dev(core=1 - core)
    mine = pl.multiple_of(core * HALF, 16)
    theirs = pl.multiple_of((1 - core) * HALF, 16)

    def put(k, part):
        for j in range(3):
            U[k, j * TOK : (j + 1) * TOK, :] = part[:, j * 128 : (j + 1) * 128].astype(BF)
        U[k, 3 * TOK :, :] = jnp.zeros((2 * HALF - 3 * TOK, 128), BF)
        send(("core", k), U.at[k, pl.ds(theirs, HALF)], RA.at[k], other)

    def chip_sum(k):
        recv(("core", k), RA.at[k])
        S[k] = (U[k, pl.ds(mine, HALF), :].astype(F32) + RA[k].astype(F32)).astype(BF)
        for d in range(1, NZ):
            zz = up(z, d, NZ)
            send(("z", k, d), S.at[k, pl.ds(pl.multiple_of(zz * SEG, 16), SEG)], RB.at[d - 1, k], dev(z=zz))

    forward(0)
    unpack(0)
    put(0, jnp.dot(X[0], wg[...], preferred_element_type=F32))
    put(1, jnp.dot(X[0], wu[...], preferred_element_type=F32))
    forward(1)
    chip_sum(0)
    chip_sum(1)
    unpack(1)
    put(2, nt(X[1], wd[...]))
    chip_sum(2)

    own = pl.multiple_of(z * SEG, 16)

    def total(k):
        t = S[k, pl.ds(own, SEG), :].astype(F32)
        for d in range(1, NZ):
            recv(("z", k, d), RB.at[d - 1, k])
            t = t + RB[d - 1, k].astype(F32)
        return t

    gate = total(0)
    up_value = total(1)
    grad_hidden = total(2)
    sig = jax.nn.sigmoid(gate)
    act = gate * sig
    at = pl.ds(pl.multiple_of(core * HALF + z * SEG, 16), SEG)
    HH[0, at, :] = (grad_hidden * up_value * sig * (1.0 + gate * (1.0 - sig))).astype(BF)
    HH[1, at, :] = (grad_hidden * act).astype(BF)
    HH[2, at, :] = (act * up_value).astype(BF)

    groups = ((0, 2), (2, 1))
    for k, (lo, n) in enumerate(groups):
        seg = HH.at[pl.ds(lo, n), at]
        for d in range(1, NZ):
            send(("back", k, d), seg, seg, dev(z=up(z, d, NZ)))
        send(("backcore", k, 0), seg, seg, other)

    def spread(k):
        lo, n = groups[k]
        for d in range(1, NZ):
            zz = wrap(z - d, NZ)
            seg = HH.at[pl.ds(lo, n), pl.ds(pl.multiple_of(core * HALF + zz * SEG, 16), SEG)]
            recv(("back", k, d), seg)
            send(("backcore", k, d), seg, seg, other)

    def collect(k):
        lo, n = groups[k]
        for d in range(NZ):
            zz = wrap(z - d, NZ)
            recv(("backcore", k, d), HH.at[pl.ds(lo, n), pl.ds(pl.multiple_of((1 - core) * HALF + zz * SEG, 16), SEG)])

    def whole(k):
        return jnp.concatenate([HH[k, j * TOK : (j + 1) * TOK, :] for j in range(3)], axis=1)

    spread(0)
    collect(0)
    ggp, gup = whole(0), whole(1)
    for n in range(4):
        rows = slice(n * 256, (n + 1) * 256)
        part = nt(ggp, wg[rows, :]) + nt(gup, wu[rows, :])
        for h in range(2):
            T[pl.ds(n * 2 + h, TOK, stride=8), :] = part[:, h * 128 : (h + 1) * 128]

    @pl.loop(0, NY)
    def _(yy):
        for xx in range(NX):
            TB[xx, yy] = T[pl.ds(pl.multiple_of((yy * 4 + xx) * 72, 8), 72), :].astype(BF)

    send(("x2r",), TB.at[xo, 0:4], RXa, right)
    send(("x2l",), TB.at[xo, 4:8], RXb, left)
    send(("x1r",), TB.at[xr, 4:8], RX1.at[4:8], right)
    send(("x1l",), TB.at[xl, 0:4], RX2.at[0:4], left)

    spread(1)

    def mine_of(yy, xx):
        return T[pl.ds(pl.multiple_of((yy * 4 + xx) * 72, 8), 72), :]

    recv(("x2r",), RXa)
    for i in range(4):
        CA[i] = (mine_of(i, xr) + RXa[i].astype(F32)).astype(BF)
    send(("xcr",), CA, RX1.at[0:4], right)
    recv(("x2l",), RXb)
    for i in range(4):
        CB[i] = (mine_of(4 + i, xl) + RXb[i].astype(F32)).astype(BF)
    send(("xcl",), CB, RX2.at[4:8], left)

    both = jnp.concatenate([ggp, gup], axis=1)
    stores = []

    def store(src, dst):
        c = pltpu.make_async_copy(src, dst, lsem.at[3 + len(stores)])
        c.start()
        stores.append(c)

    for n in range(4):
        rows = slice(n * 256, (n + 1) * 256)
        part = tn(X[0, :, rows], both)
        og[rows, :] = part[:, :HID].astype(BF)
        ou[rows, :] = part[:, HID:].astype(BF)
    store(og, gg)
    store(ou, gu)

    recv(("x1r",), RX1.at[4:8])
    recv(("x1l",), RX2.at[0:4])
    recv(("xcr",), RX1.at[0:4])
    recv(("xcl",), RX2.at[4:8])
    for i in range(NY):
        v = mine_of(i, x) + RX1[i].astype(F32) + RX2[i].astype(F32)
        YF[i] = v
        YB[i] = v.astype(BF)
    for d in range(1, NY):
        yy = up(y, d, NY)
        send(("sy", d), YB.at[yy], RY.at[d - 1], dev(y=yy))

    collect(1)
    hid = whole(2)
    for n in range(3):
        rows = slice(n * 128, (n + 1) * 128)
        od[rows, :] = tn(hid[:, rows], X[1]).astype(BF)
    store(od, gd)

    v = YF[y]
    for d in range(1, NY):
        recv(("sy", d), RY.at[d - 1])
        v = v + RY[d - 1].astype(F32)
    for i in range(NZH):
        ZB[i] = v[i * 24 : (i + 1) * 24, :]
    for d in (1, 2):
        zz = up(zh, d, 3)
        send(("sz", d), ZB.at[zz], RZ.at[d - 1], dev(zh=zz))
    v = ZB[zh]
    for d in (1, 2):
        recv(("sz", d), RZ.at[d - 1])
        v = v + RZ[d - 1]
    for r in range(3):
        for c in range(8):
            fin[r : r + 1, c * 128 : (c + 1) * 128] = v[r * 8 + c : r * 8 + c + 1, :]
    gt[...] = fin[0:3, :].astype(BF)

    for c in stores:
        c.wait()
    for c in sent:
        c.wait_send()


def local(*args):
    vmem = pl.BlockSpec(memory_space=pltpu.VMEM)
    smem = pl.BlockSpec(memory_space=pltpu.SMEM)
    hbm = pl.BlockSpec(memory_space=pl.ANY)
    V = pltpu.VMEM
    return pl.pallas_call(
        kernel,
        out_shape=(
            jax.ShapeDtypeStruct((3, FEAT), BF),
            jax.ShapeDtypeStruct((FEAT, HID), BF),
            jax.ShapeDtypeStruct((FEAT, HID), BF),
            jax.ShapeDtypeStruct((HID, FEAT), BF),
        ),
        in_specs=[vmem, vmem, hbm, smem, hbm, smem, hbm, smem],
        out_specs=(vmem, hbm, hbm, hbm),
        scratch_shapes=[
            V((FEAT, HID), BF), V((FEAT, HID), BF), V((HID, FEAT), BF),
            V((2, NY, NX, NZH, 24, 128), BF),
            V((TOK * 8, 128), F32),
            V((2, TOK, FEAT), BF),
            V((3, 2 * HALF, 128), BF),
            V((3, HALF, 128), BF),
            V((3, HALF, 128), BF),
            V((3, 3, SEG, 128), BF),
            V((3, 2 * HALF, 128), BF),
            V((TOK * 8, 128), F32),
            V((NX, NY, 72, 128), BF),
            V((NY, 72, 128), BF), V((NY, 72, 128), BF),
            V((4, 72, 128), BF), V((4, 72, 128), BF),
            V((4, 72, 128), BF), V((4, 72, 128), BF),
            V((NY, 72, 128), BF), V((NY, 72, 128), F32), V((NY - 1, 72, 128), BF),
            V((NZH, 24, 128), F32), V((2, 24, 128), F32),
            V((FEAT, HID), BF), V((FEAT, HID), BF), V((HID, FEAT), BF),
            V((8, FEAT), F32),
            pltpu.SemaphoreType.DMA((6,)),
            pltpu.SemaphoreType.DMA((N_IDS,)),
            pltpu.SemaphoreType.DMA((N_IDS,)),
        ],
        compiler_params=pltpu.CompilerParams(
            collective_id=0, has_side_effects=True, vmem_limit_bytes=48 * 1024 * 1024
        ),
    )(*args)


def solution(mesh):
    return jax.shard_map(
        local,
        mesh=mesh,
        in_specs=(
            P("fsdp", "tp"),
            P("fsdp", "tp"),
            P("tp", "fsdp"),
            P("tp", "fsdp"),
            P("tp", "fsdp"),
            P("tp", "fsdp"),
            P("fsdp", "tp"),
            P("fsdp", "tp"),
        ),
        out_specs=(P("fsdp", "tp"), P("tp", "fsdp"), P("tp", "fsdp"), P("fsdp", "tp")),
        check_vma=False,
    )
```

```python
import functools

import jax
import jax.numpy as jnp
from jax import lax
from jax.experimental import pallas as pl
from jax.experimental.pallas import tpu as pltpu
from jax.sharding import PartitionSpec as P

BF = jnp.bfloat16
F32 = jnp.float32
NY, NX, NZH, NZ = 8, 4, 3, 4
TOK, FEAT, HID = 288, 1024, 384
MESH = pl.DeviceIdType.MESH

NB = (1, 2)
NT = (96, 192)
FIRST = (0, 96)
SEG = (48, 80)
HALF = (192, 320)

_IDS = {}


def _id(*key):
    return _IDS.setdefault(key, len(_IDS))


for _d in (1, 2):
    _id("gz", _d)
    _id("sz", _d)
for _h in range(2):
    for _d in range(1, NY):
        _id("gy", _h, _d)
        _id("sy", _h, _d)
    for _k in ("gxr", "gxl", "gxr2", "gxl2", "core", "x2r", "x2l", "x1r", "x1l", "xcr", "xcl"):
        _id(_k, _h)
    for _d in range(1, NZ):
        _id("z", _h, _d)
for _k in range(3):
    for _d in range(NZ):
        _id("back", _k, _d)
        _id("backcore", _k, _d)
N_IDS = len(_IDS)


def nt(left, right):
    return lax.dot_general(left, right, (((1,), (1,)), ((), ())), preferred_element_type=F32)


def tn(left, right):
    return lax.dot_general(left, right, (((0,), (0,)), ((), ())), preferred_element_type=F32)


def kernel(
    tok_in, gout_in, gc, gs_in, uc, us_in, dc, ds_in,
    gt, gg, gu, gd,
    tok, gout, gs, us, dsc, wg, wu, wd, X, og, ou, od, fin, ZB, RZ,
    *rest,
):
    per, (lsem, ssem, rsem) = (rest[:19], rest[19:38]), rest[38:]
    G, st, U, UB, RA, S, RB, HH, T, TB, RX1, RX2, RXa, RXb, CA, CB, YB, YF, RY = zip(*per)

    f = lax.axis_index("fsdp")
    tp = lax.axis_index("tp")
    y, zh, x = f // 12, lax.rem(f // 4, 3), lax.rem(f, 4)
    z, core = tp // 2, lax.rem(tp, 2)

    def dev(y=y, zh=zh, x=x, z=z, core=core):
        return ((y * 3 + zh) * 4 + x, z * 2 + core)

    def up(v, d, n):
        return lax.rem(v + n + d, n)

    def rcopy(key, src, dst, to):
        i = _IDS[key]
        return pltpu.make_async_remote_copy(
            src_ref=src, dst_ref=dst, send_sem=ssem.at[i], recv_sem=rsem.at[i],
            device_id=to, device_id_type=MESH,
        )

    sent = []

    def send(key, src, dst, to):
        c = rcopy(key, src, dst, to)
        c.start()
        sent.append(c)

    def recv(key, dst):
        rcopy(key, dst, dst, dev(core=1 - core)).wait_recv()

    barrier = pltpu.get_barrier_semaphore()
    partners = (
        [dev(y=up(y, d, NY)) for d in range(1, NY)]
        + [dev(zh=up(zh, d, 3)) for d in (1, 2)]
        + [dev(x=up(x, d, NX)) for d in (1, 3)]
        + [dev(z=up(z, d, NZ)) for d in range(1, NZ)]
        + [dev(core=1 - core)]
    )
    for p in partners:
        pl.semaphore_signal(barrier, inc=1, device_id=p, device_id_type=MESH)

    loads = [
        pltpu.make_async_copy(s, d, lsem.at[i])
        for i, (s, d) in enumerate((
            (gc, wg), (uc, wu), (dc, wd), (tok_in, tok), (gout_in, gout), (gs_in, gs), (us_in, us), (ds_in, dsc),
        ))
    ]
    for i in (3, 4, 5, 0, 6, 1, 7, 2):
        loads[i].start()

    for a, ref in ((0, tok), (1, gout)):
        loads[3 + a].wait()
        v = ref[...].astype(F32)
        for r in range(3):
            for c in range(8):
                st[0][a * 24 + r * 8 + c : a * 24 + r * 8 + c + 1, :] = v[r : r + 1, c * 128 : (c + 1) * 128]
        G[0][0, 0, 0, a] = st[0][a * 24 : (a + 1) * 24, :].astype(BF)

    pl.semaphore_wait(barrier, len(partners))

    def spread_y(h):
        for d in (4, 3, 5, 2, 6, 1, 7):
            send(("gy", h, d), G[h].at[0, 0], G[h].at[0, d], dev(y=up(y, d, NY)))

    right, left = dev(x=up(x, 1, NX)), dev(x=up(x, 3, NX))
    other = dev(core=1 - core)

    def spread_x(h):
        for d in range(1, NY):
            recv(("gy", h, d), G[h].at[0, d])
        send(("gxr", h), G[h].at[0], G[h].at[1], right)
        send(("gxl", h), G[h].at[0], G[h].at[2], left)

    def forward(h):
        recv(("gxr", h), G[h].at[1])
        send(("gxr2", h), G[h].at[1, 0:4], G[h].at[3, 0:4], right)
        recv(("gxl", h), G[h].at[2])
        send(("gxl2", h), G[h].at[2, 4:8], G[h].at[3, 4:8], left)

    def gathered(h):
        recv(("gxr2", h), G[h].at[3, 0:4])
        recv(("gxl2", h), G[h].at[3, 4:8])

    def dequant(i, w, sc):
        loads[i].wait()
        loads[5 + i].wait()
        nr, nc = w.shape[0] // 128, w.shape[1] // 128
        for r in range(nr):
            for c in range(nc):
                t = w[r * 128 : (r + 1) * 128, c * 128 : (c + 1) * 128]
                w[r * 128 : (r + 1) * 128, c * 128 : (c + 1) * 128] = (t.astype(F32) * (sc[c, r] if i < 2 else sc[r, c])).astype(BF)

    def tokens_of(h):
        return slice(FIRST[h], FIRST[h] + NT[h])

    def unpack(h, a):
        n = 192 * NB[h]
        for slot in range(NX):
            for k in range(NB[h]):
                for d in range(NY):
                    row = slot * n + (d * NB[h] + k) * 24
                    st[h][row : row + 24, :] = G[h][slot, d, k, a].astype(F32)
        for c in range(8):
            X[a, tokens_of(h), c * 128 : (c + 1) * 128] = st[h][pl.ds(c, NT[h], stride=8), :].astype(BF)

    def put(h, k, part):
        for j in range(3):
            U[h][k, j * NT[h] : (j + 1) * NT[h], :] = part[:, j * 128 : (j + 1) * 128]

    def rows(start, n):
        return pl.ds(pl.multiple_of(start, 16), n)

    def hand(h):
        unpack(h, 0)
        put(h, 0, jnp.dot(X[0, tokens_of(h), :], wg[...], preferred_element_type=F32))
        put(h, 1, jnp.dot(X[0, tokens_of(h), :], wu[...], preferred_element_type=F32))
        unpack(h, 1)
        put(h, 2, nt(X[1, tokens_of(h), :], wd[...]))
        for k in range(3):
            UB[h][k] = U[h][k, rows((1 - core) * HALF[h], HALF[h]), :].astype(BF)
        send(("core", h), UB[h], RA[h], other)

    def chip_sum(h):
        recv(("core", h), RA[h])
        for k in range(3):
            S[h][k] = (U[h][k, rows(core * HALF[h], HALF[h]), :] + RA[h][k].astype(F32)).astype(BF)
        for d in (2, 1, 3):
            zz = up(z, d, NZ)
            send(("z", h, d), S[h].at[:, rows(zz * SEG[h], SEG[h])], RB[h].at[d - 1], dev(z=zz))

    def share(h, zz, cc):
        return rows(cc * HALF[h] + zz * SEG[h], SEG[h])

    def middle(h):
        for d in range(1, NZ):
            recv(("z", h, d), RB[h].at[d - 1])

        def total(k):
            t = U[h][k, share(h, z, core), :] + RA[h][k, rows(z * SEG[h], SEG[h]), :].astype(F32)
            for d in range(1, NZ):
                t = t + RB[h][d - 1, k].astype(F32)
            return t

        gate, up_value, grad_hidden = total(0), total(1), total(2)
        sig = jax.nn.sigmoid(gate)
        act = gate * sig
        at = share(h, z, core)
        HH[h][0, at, :] = (grad_hidden * up_value * sig * (1.0 + gate * (1.0 - sig))).astype(BF)
        HH[h][1, at, :] = (grad_hidden * act).astype(BF)
        HH[h][2, at, :] = (act * up_value).astype(BF)

    groups = ((0, 0, 3), (1, 0, 2), (1, 2, 1))

    def piece(g, zz, cc):
        h, lo, n = groups[g]
        return HH[h].at[pl.ds(lo, n), share(h, zz, cc)]

    def give(g):
        seg = piece(g, z, core)
        for d in (2, 1, 3):
            send(("back", g, d), seg, seg, dev(z=up(z, d, NZ)))
        send(("backcore", g, 0), seg, seg, other)

    def spread(g):
        for d in (1, 3, 2):
            seg = piece(g, up(z, -d, NZ), core)
            recv(("back", g, d), seg)
            send(("backcore", g, d), seg, seg, other)

    def collect(g):
        for d in range(NZ):
            recv(("backcore", g, d), piece(g, up(z, -d, NZ), 1 - core))

    def whole(h, k):
        return jnp.concatenate([HH[h][k, j * NT[h] : (j + 1) * NT[h], :] for j in range(3)], axis=1)

    def input_grad(h):
        ggp, gup = whole(h, 0), whole(h, 1)
        for n in range(4):
            r = slice(n * 256, (n + 1) * 256)
            part = nt(ggp, wg[r, :]) + nt(gup, wu[r, :])
            for q in range(2):
                T[h][pl.ds(n * 2 + q, NT[h], stride=8), :] = part[:, q * 128 : (q + 1) * 128]

    def slab(h, p, lo, hi):
        n = 24 * NB[h]
        return T[h][(p * 8 + lo) * n : (p * 8 + hi) * n, :].reshape(hi - lo, n, 128)

    def sum_x(h):
        TB[h][3] = slab(h, 3, 0, 8).astype(BF)
        send(("x2r", h), TB[h].at[3, 0:4], RXa[h], right)
        send(("x2l", h), TB[h].at[3, 4:8], RXb[h], left)
        TB[h][2, 4:8] = slab(h, 2, 4, 8).astype(BF)
        TB[h][1, 0:4] = slab(h, 1, 0, 4).astype(BF)
        send(("x1r", h), TB[h].at[2, 4:8], RX1[h].at[4:8], right)
        send(("x1l", h), TB[h].at[1, 0:4], RX2[h].at[0:4], left)

    def sum_x2(h):
        recv(("x2r", h), RXa[h])
        CA[h][...] = (slab(h, 2, 0, 4) + RXa[h][...].astype(F32)).astype(BF)
        send(("xcr", h), CA[h], RX1[h].at[0:4], right)
        recv(("x2l", h), RXb[h])
        CB[h][...] = (slab(h, 1, 4, 8) + RXb[h][...].astype(F32)).astype(BF)
        send(("xcl", h), CB[h], RX2[h].at[4:8], left)

    def sum_y(h):
        recv(("x1r", h), RX1[h].at[4:8])
        recv(("x1l", h), RX2[h].at[0:4])
        recv(("xcr", h), RX1[h].at[0:4])
        recv(("xcl", h), RX2[h].at[4:8])
        n = 24 * NB[h]
        for d in (4, 3, 5, 2, 6, 1, 7, 0):
            v = T[h][d * n : (d + 1) * n, :] + RX1[h][d].astype(F32) + RX2[h][d].astype(F32)
            if d:
                YB[h][d] = v.astype(BF)
                send(("sy", h, d), YB[h].at[d], RY[h].at[d - 1], dev(y=up(y, -d, NY)))
            else:
                YF[h][...] = v

    def summed_y(h):
        v = YF[h][...]
        for d in (1, 7, 2, 6, 3, 5, 4):
            recv(("sy", h, d), RY[h].at[d - 1])
            v = v + RY[h][d - 1].astype(F32)
        return v

    stores = []

    def store(src, dst):
        c = pltpu.make_async_copy(src, dst, lsem.at[8 + len(stores)])
        c.start()
        stores.append(c)

    for d in (1, 2):
        send(("gz", d), G[0].at[0, 0, 0], G[1].at[0, 0, d - 1], dev(zh=up(zh, d, 3)))
    spread_y(0)
    for h in range(2):
        for k in range(3):
            U[h][k, 3 * NT[h] :, :] = jnp.zeros((2 * HALF[h] - 3 * NT[h], 128), F32)
    dequant(0, wg, gs)
    dequant(1, wu, us)
    dequant(2, wd, dsc)
    for d in (1, 2):
        recv(("gz", d), G[1].at[0, 0, d - 1])
    spread_y(1)
    spread_x(0)
    forward(0)
    gathered(0)
    hand(0)
    spread_x(1)
    chip_sum(0)
    forward(1)
    middle(0)
    give(0)
    gathered(1)
    hand(1)
    spread(0)
    chip_sum(1)
    collect(0)
    input_grad(0)
    sum_x(0)
    sum_x2(0)
    middle(1)
    give(1)
    sum_y(0)
    spread(1)
    give(2)
    collect(1)
    input_grad(1)
    sum_x(1)
    own_sum = summed_y(0)
    fin[0:24, 0:128] = own_sum
    sum_x2(1)
    spread(2)

    both = jnp.concatenate(
        [jnp.concatenate([whole(h, 0), whole(h, 1)], axis=1) for h in range(2)], axis=0
    )

    def weight_grads(n):
        r = slice(n * 256, (n + 1) * 256)
        part = tn(X[0, :, r], both)
        og[r, :] = part[:, :HID].astype(BF)
        ou[r, :] = part[:, HID:].astype(BF)

    weight_grads(0)
    weight_grads(1)
    sum_y(1)
    weight_grads(2)
    weight_grads(3)
    store(og, gg)
    store(ou, gu)
    collect(2)
    hid = jnp.concatenate([whole(0, 2), whole(1, 2)], axis=0)
    for n in range(3):
        r = slice(n * 128, (n + 1) * 128)
        od[r, :] = tn(hid[:, r], X[1]).astype(BF)
    store(od, gd)

    v = summed_y(1)
    for i in range(2):
        ZB[i] = v[i * 24 : (i + 1) * 24, :]
    for d in (1, 2):
        send(("sz", d), ZB.at[d - 1], RZ.at[d - 1], dev(zh=up(zh, -d, 3)))
    v = fin[0:24, 0:128]
    for d in (1, 2):
        recv(("sz", d), RZ.at[d - 1])
        v = v + RZ[d - 1]
    for r in range(3):
        for c in range(8):
            fin[r : r + 1, c * 128 : (c + 1) * 128] = v[r * 8 + c : r * 8 + c + 1, :]
    gt[...] = fin[0:3, :].astype(BF)

    for c in stores:
        c.wait()
    for c in sent:
        c.wait_send()


def copies(*refs):
    ins, outs, bufs, isem, osem = refs[:4], refs[4:8], refs[8:12], refs[12], refs[13]
    parts = []
    for i in range(4):
        rows = ins[i].shape[0]
        n = 2 if i else 1
        parts += [(i, slice(j * rows // n, (j + 1) * rows // n)) for j in range(n)]
    loads = [pltpu.make_async_copy(ins[i].at[r], bufs[i].at[r], isem.at[k]) for k, (i, r) in enumerate(parts)]
    stores = [pltpu.make_async_copy(bufs[i].at[r], outs[i].at[r], osem.at[k]) for k, (i, r) in enumerate(parts)]
    for c in loads:
        c.start()
    for k, c in enumerate(loads):
        c.wait()
        stores[k].start()
    for c in stores:
        c.wait()


def chunk_scratch(h):
    V = pltpu.VMEM
    n, half, seg = 24 * NB[h], HALF[h], SEG[h]
    return [
        V((NX, NY, NB[h], 2, 24, 128), BF),
        V((NT[h] * 8, 128), F32),
        V((3, 2 * half, 128), F32),
        V((3, half, 128), BF), V((3, half, 128), BF), V((3, half, 128), BF),
        V((NZ - 1, 3, seg, 128), BF),
        V((3, 2 * half, 128), BF),
        V((NT[h] * 8, 128), F32),
        V((NX, NY, n, 128), BF),
        V((NY, n, 128), BF), V((NY, n, 128), BF),
        V((4, n, 128), BF), V((4, n, 128), BF), V((4, n, 128), BF), V((4, n, 128), BF),
        V((NY, n, 128), BF), V((n, 128), F32), V((NY - 1, n, 128), BF),
    ]


def local(tokens, grad_out, gate_codes, gate_scale, up_codes, up_scale, down_codes, down_scale):
    vmem = pl.BlockSpec(memory_space=pltpu.VMEM)
    hbm = pl.BlockSpec(memory_space=pl.ANY)
    V = pltpu.VMEM
    far = pl.BlockSpec(memory_space=pltpu.HBM)
    shapes = (
        jax.ShapeDtypeStruct((3, FEAT), BF),
        jax.ShapeDtypeStruct((FEAT, HID), BF),
        jax.ShapeDtypeStruct((FEAT, HID), BF),
        jax.ShapeDtypeStruct((HID, FEAT), BF),
    )
    results = pl.pallas_call(
        kernel,
        out_shape=shapes,
        in_specs=[far] * 8,
        out_specs=(vmem, hbm, hbm, hbm),
        scratch_shapes=[
            V((3, FEAT), BF), V((3, FEAT), BF),
            pltpu.SMEM((3, 8), F32), pltpu.SMEM((3, 8), F32), pltpu.SMEM((3, 8), F32),
            V((FEAT, HID), BF), V((FEAT, HID), BF), V((HID, FEAT), BF),
            V((2, TOK, FEAT), BF),
            V((FEAT, HID), BF), V((FEAT, HID), BF), V((HID, FEAT), BF),
            V((24, FEAT), F32),
            V((2, 24, 128), F32), V((2, 24, 128), F32),
            *chunk_scratch(0), *chunk_scratch(1),
            pltpu.SemaphoreType.DMA((11,)),
            pltpu.SemaphoreType.DMA((N_IDS,)),
            pltpu.SemaphoreType.DMA((N_IDS,)),
        ],
        compiler_params=pltpu.CompilerParams(
            collective_id=0, has_side_effects=True, vmem_limit_bytes=63 * 1024 * 1024
        ),
    )(tokens, grad_out, gate_codes, gate_scale.T, up_codes, up_scale.T, down_codes, down_scale)
    return pl.pallas_call(
        copies,
        out_shape=shapes,
        in_specs=[hbm] * 4,
        out_specs=(far,) * 4,
        scratch_shapes=[V(a.shape, BF) for a in shapes]
        + [pltpu.SemaphoreType.DMA((7,)), pltpu.SemaphoreType.DMA((7,))],
        compiler_params=pltpu.CompilerParams(vmem_limit_bytes=63 * 1024 * 1024),
    )(*results)


def solution(mesh):
    return jax.shard_map(
        local,
        mesh=mesh,
        in_specs=(
            P("fsdp", "tp"),
            P("fsdp", "tp"),
            P("tp", "fsdp"),
            P("tp", "fsdp"),
            P("tp", "fsdp"),
            P("tp", "fsdp"),
            P("fsdp", "tp"),
            P("fsdp", "tp"),
        ),
        out_specs=(P("fsdp", "tp"), P("tp", "fsdp"), P("tp", "fsdp"), P("fsdp", "tp")),
        check_vma=False,
    )
```

```python
import functools

import jax
import jax.numpy as jnp
from jax import lax
from jax.experimental import pallas as pl
from jax.experimental.pallas import tpu as pltpu
from jax.sharding import PartitionSpec as P

BF = jnp.bfloat16
F32 = jnp.float32
NY, NX, NZH, NZ = 8, 4, 3, 4
TOK, FEAT, HID = 288, 1024, 384
MESH = pl.DeviceIdType.MESH

NB = (1, 2)
NT = (96, 192)
FIRST = (0, 96)
SEG = (48, 80)
HALF = (192, 320)

_IDS = {}


def _id(*key):
    return _IDS.setdefault(key, len(_IDS))


for _d in (1, 2):
    _id("gz", _d)
    _id("sz", _d)
for _h in range(2):
    for _d in range(1, NY):
        _id("gy", _h, _d)
        _id("sy", _h, _d)
    for _k in ("gxr", "gxl", "gxr2", "gxl2", "gxrb", "gxlb", "core", "x2r", "x2l", "x1r", "x1l", "xcr", "xcl"):
        _id(_k, _h)
    for _d in range(1, NZ):
        _id("z", _h, _d)
for _k in range(3):
    for _d in range(NZ):
        _id("back", _k, _d)
        _id("backcore", _k, _d)
N_IDS = len(_IDS)


def nt(left, right):
    return lax.dot_general(left, right, (((1,), (1,)), ((), ())), preferred_element_type=F32)


def tn(left, right):
    return lax.dot_general(left, right, (((0,), (0,)), ((), ())), preferred_element_type=F32)


def kernel(
    tok_in, gout_in, gc, gs_in, uc, us_in, dc, ds_in,
    gt, gg, gu, gd,
    tok, gout, gs, us, dsc, wg, wu, wd, X, og, ou, od, fin, ZB, RZ,
    *rest,
):
    per, (lsem, ssem, rsem) = (rest[:19], rest[19:38]), rest[38:]
    G, st, U, UB, RA, S, RB, HH, T, TB, RX1, RX2, RXa, RXb, CA, CB, YB, YF, RY = zip(*per)

    f = lax.axis_index("fsdp")
    tp = lax.axis_index("tp")
    y, zh, x = f // 12, lax.rem(f // 4, 3), lax.rem(f, 4)
    z, core = tp // 2, lax.rem(tp, 2)

    def dev(y=y, zh=zh, x=x, z=z, core=core):
        return ((y * 3 + zh) * 4 + x, z * 2 + core)

    def up(v, d, n):
        return lax.rem(v + n + d, n)

    def rcopy(key, src, dst, to):
        i = _IDS[key]
        return pltpu.make_async_remote_copy(
            src_ref=src, dst_ref=dst, send_sem=ssem.at[i], recv_sem=rsem.at[i],
            device_id=to, device_id_type=MESH,
        )

    sent = []

    def send(key, src, dst, to):
        c = rcopy(key, src, dst, to)
        c.start()
        sent.append(c)

    def gone(n):
        for c in sent[-n:]:
            c.wait_send()
        del sent[-n:]

    def recv(key, dst):
        rcopy(key, dst, dst, dev(core=1 - core)).wait_recv()

    barrier = pltpu.get_barrier_semaphore()
    partners = (
        [dev(y=up(y, d, NY)) for d in range(1, NY)]
        + [dev(zh=up(zh, d, 3)) for d in (1, 2)]
        + [dev(x=up(x, d, NX)) for d in (1, 3)]
        + [dev(z=up(z, d, NZ)) for d in range(1, NZ)]
        + [dev(core=1 - core)]
    )
    for p in partners:
        pl.semaphore_signal(barrier, inc=1, device_id=p, device_id_type=MESH)

    loads = [
        pltpu.make_async_copy(s, d, lsem.at[i])
        for i, (s, d) in enumerate((
            (gc, wg), (uc, wu), (dc, wd), (tok_in, tok), (gout_in, gout), (gs_in, gs), (us_in, us), (ds_in, dsc),
        ))
    ]
    for i in (3, 4, 5, 0, 6, 1, 7, 2):
        loads[i].start()

    for a, ref in ((0, tok), (1, gout)):
        loads[3 + a].wait()
        v = ref[...].astype(F32)
        for r in range(3):
            for c in range(8):
                st[0][a * 24 + r * 8 + c : a * 24 + r * 8 + c + 1, :] = v[r : r + 1, c * 128 : (c + 1) * 128]
        G[0][0, 0, 0, a] = st[0][a * 24 : (a + 1) * 24, :].astype(BF)

    pl.semaphore_wait(barrier, len(partners))

    def spread_y(h):
        for d in (4, 3, 5, 2, 6, 1, 7):
            send(("gy", h, d), G[h].at[0, 0], G[h].at[0, d], dev(y=up(y, d, NY)))

    right, left = dev(x=up(x, 1, NX)), dev(x=up(x, 3, NX))
    other = dev(core=1 - core)

    def spread_x(h):
        for d in range(1, NY):
            recv(("gy", h, d), G[h].at[0, d])
        send(("gxr", h), G[h].at[0, 0:4], G[h].at[1, 0:4], right)
        send(("gxl", h), G[h].at[0, 4:8], G[h].at[2, 4:8], left)

    def spread_x2(h):
        send(("gxrb", h), G[h].at[0, 4:8], G[h].at[1, 4:8], right)
        send(("gxlb", h), G[h].at[0, 0:4], G[h].at[2, 0:4], left)

    def forward(h):
        recv(("gxr", h), G[h].at[1, 0:4])
        send(("gxr2", h), G[h].at[1, 0:4], G[h].at[3, 0:4], right)
        recv(("gxl", h), G[h].at[2, 4:8])
        send(("gxl2", h), G[h].at[2, 4:8], G[h].at[3, 4:8], left)

    def gathered(h):
        recv(("gxrb", h), G[h].at[1, 4:8])
        recv(("gxlb", h), G[h].at[2, 0:4])
        recv(("gxr2", h), G[h].at[3, 0:4])
        recv(("gxl2", h), G[h].at[3, 4:8])

    def dequant(i, w, sc):
        loads[i].wait()
        loads[5 + i].wait()
        nr, nc = w.shape[0] // 128, w.shape[1] // 128
        for r in range(nr):
            for c in range(nc):
                t = w[r * 128 : (r + 1) * 128, c * 128 : (c + 1) * 128]
                w[r * 128 : (r + 1) * 128, c * 128 : (c + 1) * 128] = (t.astype(F32) * (sc[c, r] if i < 2 else sc[r, c])).astype(BF)

    def tokens_of(h):
        return slice(FIRST[h], FIRST[h] + NT[h])

    def unpack(h, a):
        n = 192 * NB[h]
        for slot in range(NX):
            for k in range(NB[h]):
                for d in range(NY):
                    row = slot * n + (d * NB[h] + k) * 24
                    st[h][row : row + 24, :] = G[h][slot, d, k, a].astype(F32)
        for c in range(8):
            X[a, tokens_of(h), c * 128 : (c + 1) * 128] = st[h][pl.ds(c, NT[h], stride=8), :].astype(BF)

    def put(h, k, part):
        for j in range(3):
            U[h][k, j * NT[h] : (j + 1) * NT[h], :] = part[:, j * 128 : (j + 1) * 128]

    def rows(start, n):
        return pl.ds(pl.multiple_of(start, 16), n)

    def hand(h):
        unpack(h, 0)
        put(h, 0, jnp.dot(X[0, tokens_of(h), :], wg[...], preferred_element_type=F32))
        put(h, 1, jnp.dot(X[0, tokens_of(h), :], wu[...], preferred_element_type=F32))
        unpack(h, 1)
        put(h, 2, nt(X[1, tokens_of(h), :], wd[...]))
        for k in range(3):
            UB[h][k] = U[h][k, rows((1 - core) * HALF[h], HALF[h]), :].astype(BF)
        send(("core", h), UB[h], RA[h], other)

    def chip_sum(h):
        recv(("core", h), RA[h])
        for k in range(3):
            S[h][k] = (U[h][k, rows(core * HALF[h], HALF[h]), :] + RA[h][k].astype(F32)).astype(BF)
        for d in (2, 1, 3):
            zz = up(z, d, NZ)
            send(("z", h, d), S[h].at[:, rows(zz * SEG[h], SEG[h])], RB[h].at[d - 1], dev(z=zz))

    def share(h, zz, cc):
        return rows(cc * HALF[h] + zz * SEG[h], SEG[h])

    def middle(h):
        for d in range(1, NZ):
            recv(("z", h, d), RB[h].at[d - 1])

        def total(k):
            t = U[h][k, share(h, z, core), :] + RA[h][k, rows(z * SEG[h], SEG[h]), :].astype(F32)
            for d in range(1, NZ):
                t = t + RB[h][d - 1, k].astype(F32)
            return t

        gate, up_value, grad_hidden = total(0), total(1), total(2)
        sig = jax.nn.sigmoid(gate)
        act = gate * sig
        at = share(h, z, core)
        HH[h][0, at, :] = (grad_hidden * up_value * sig * (1.0 + gate * (1.0 - sig))).astype(BF)
        HH[h][1, at, :] = (grad_hidden * act).astype(BF)
        HH[h][2, at, :] = (act * up_value).astype(BF)

    groups = ((0, 0, 3), (1, 0, 2), (1, 2, 1))

    def piece(g, zz, cc):
        h, lo, n = groups[g]
        return HH[h].at[pl.ds(lo, n), share(h, zz, cc)]

    def give(g):
        seg = piece(g, z, core)
        for d in (2, 1, 3):
            send(("back", g, d), seg, seg, dev(z=up(z, d, NZ)))
        send(("backcore", g, 0), seg, seg, other)

    def spread(g):
        for d in (1, 3, 2):
            seg = piece(g, up(z, -d, NZ), core)
            recv(("back", g, d), seg)
            send(("backcore", g, d), seg, seg, other)

    def collect(g):
        for d in range(NZ):
            recv(("backcore", g, d), piece(g, up(z, -d, NZ), 1 - core))

    def whole(h, k):
        return jnp.concatenate([HH[h][k, j * NT[h] : (j + 1) * NT[h], :] for j in range(3)], axis=1)

    def input_grad(h, half):
        r, start = slice(half * NT[h] // 2, (half + 1) * NT[h] // 2), half * NT[h] * 4
        ggp, gup = whole(h, 0)[r], whole(h, 1)[r]
        for n in range(4):
            w = slice(n * 256, (n + 1) * 256)
            part = nt(ggp, wg[w, :]) + nt(gup, wu[w, :])
            for q in range(2):
                T[h][pl.ds(start + n * 2 + q, NT[h] // 2, stride=8), :] = part[:, q * 128 : (q + 1) * 128]

    def slab(h, p, lo, hi):
        n = 24 * NB[h]
        return T[h][(p * 8 + lo) * n : (p * 8 + hi) * n, :].reshape(hi - lo, n, 128)

    def sum_x(h):
        input_grad(h, 1)
        TB[h][3] = slab(h, 3, 0, 8).astype(BF)
        send(("x2r", h), TB[h].at[3, 0:4], RXa[h], right)
        send(("x2l", h), TB[h].at[3, 4:8], RXb[h], left)
        input_grad(h, 0)
        TB[h][2, 4:8] = slab(h, 2, 4, 8).astype(BF)
        TB[h][1, 0:4] = slab(h, 1, 0, 4).astype(BF)
        gone(2)
        send(("x1r", h), TB[h].at[2, 4:8], RX1[h].at[4:8], right)
        send(("x1l", h), TB[h].at[1, 0:4], RX2[h].at[0:4], left)

    def sum_x2(h):
        recv(("x2r", h), RXa[h])
        CA[h][...] = (slab(h, 2, 0, 4) + RXa[h][...].astype(F32)).astype(BF)
        send(("xcr", h), CA[h], RX1[h].at[0:4], right)
        recv(("x2l", h), RXb[h])
        CB[h][...] = (slab(h, 1, 4, 8) + RXb[h][...].astype(F32)).astype(BF)
        send(("xcl", h), CB[h], RX2[h].at[4:8], left)

    def sum_y(h):
        recv(("x1r", h), RX1[h].at[4:8])
        recv(("x1l", h), RX2[h].at[0:4])
        recv(("xcr", h), RX1[h].at[0:4])
        recv(("xcl", h), RX2[h].at[4:8])
        n = 24 * NB[h]
        for d in (4, 3, 5, 2, 6, 1, 7, 0):
            v = T[h][d * n : (d + 1) * n, :] + RX1[h][d].astype(F32) + RX2[h][d].astype(F32)
            if d:
                YB[h][d] = v.astype(BF)
                send(("sy", h, d), YB[h].at[d], RY[h].at[d - 1], dev(y=up(y, -d, NY)))
            else:
                YF[h][...] = v

    def summed_y(h):
        v = YF[h][...]
        for d in (1, 7, 2, 6, 3, 5, 4):
            recv(("sy", h, d), RY[h].at[d - 1])
            v = v + RY[h][d - 1].astype(F32)
        return v

    stores = []

    def store(src, dst):
        c = pltpu.make_async_copy(src, dst, lsem.at[8 + len(stores)])
        c.start()
        stores.append(c)

    for d in (1, 2):
        send(("gz", d), G[0].at[0, 0, 0], G[1].at[0, 0, d - 1], dev(zh=up(zh, d, 3)))
    spread_y(0)
    for h in range(2):
        for k in range(3):
            U[h][k, 3 * NT[h] :, :] = jnp.zeros((2 * HALF[h] - 3 * NT[h], 128), F32)
    dequant(0, wg, gs)
    dequant(1, wu, us)
    dequant(2, wd, dsc)
    for d in (1, 2):
        recv(("gz", d), G[1].at[0, 0, d - 1])
    spread_y(1)
    spread_x(0)
    spread_x2(0)
    forward(0)
    spread_x(1)
    gathered(0)
    hand(0)
    spread_x2(1)
    chip_sum(0)
    forward(1)
    middle(0)
    give(0)
    gathered(1)
    hand(1)
    spread(0)
    chip_sum(1)
    collect(0)
    sum_x(0)
    sum_x2(0)
    middle(1)
    give(1)
    sum_y(0)
    spread(1)
    give(2)
    collect(1)
    sum_x(1)
    own_sum = summed_y(0)
    fin[0:24, 0:128] = own_sum
    sum_x2(1)
    spread(2)

    both = jnp.concatenate(
        [jnp.concatenate([whole(h, 0), whole(h, 1)], axis=1) for h in range(2)], axis=0
    )

    def weight_grads(n):
        r = slice(n * 256, (n + 1) * 256)
        part = tn(X[0, :, r], both)
        og[r, :] = part[:, :HID].astype(BF)
        ou[r, :] = part[:, HID:].astype(BF)

    weight_grads(0)
    weight_grads(1)
    sum_y(1)
    weight_grads(2)
    weight_grads(3)
    store(og, gg)
    store(ou, gu)
    collect(2)
    hid = jnp.concatenate([whole(0, 2), whole(1, 2)], axis=0)
    for n in range(3):
        r = slice(n * 128, (n + 1) * 128)
        od[r, :] = tn(hid[:, r], X[1]).astype(BF)
    store(od, gd)

    v = summed_y(1)
    for i in range(2):
        ZB[i] = v[i * 24 : (i + 1) * 24, :]
    for d in (1, 2):
        send(("sz", d), ZB.at[d - 1], RZ.at[d - 1], dev(zh=up(zh, -d, 3)))
    v = fin[0:24, 0:128]
    for d in (1, 2):
        recv(("sz", d), RZ.at[d - 1])
        v = v + RZ[d - 1]
    for r in range(3):
        for c in range(8):
            fin[r : r + 1, c * 128 : (c + 1) * 128] = v[r * 8 + c : r * 8 + c + 1, :]
    gt[...] = fin[0:3, :].astype(BF)

    for c in stores:
        c.wait()
    for c in sent:
        c.wait_send()


def copies(*refs):
    ins, outs, bufs, isem, osem = refs[:4], refs[4:8], refs[8:12], refs[12], refs[13]
    parts = []
    for i in range(4):
        rows = ins[i].shape[0]
        n = 2 if i else 1
        parts += [(i, slice(j * rows // n, (j + 1) * rows // n)) for j in range(n)]
    loads = [pltpu.make_async_copy(ins[i].at[r], bufs[i].at[r], isem.at[k]) for k, (i, r) in enumerate(parts)]
    stores = [pltpu.make_async_copy(bufs[i].at[r], outs[i].at[r], osem.at[k]) for k, (i, r) in enumerate(parts)]
    for c in loads:
        c.start()
    for k, c in enumerate(loads):
        c.wait()
        stores[k].start()
    for c in stores:
        c.wait()


def chunk_scratch(h):
    V = pltpu.VMEM
    n, half, seg = 24 * NB[h], HALF[h], SEG[h]
    return [
        V((NX, NY, NB[h], 2, 24, 128), BF),
        V((NT[h] * 8, 128), F32),
        V((3, 2 * half, 128), F32),
        V((3, half, 128), BF), V((3, half, 128), BF), V((3, half, 128), BF),
        V((NZ - 1, 3, seg, 128), BF),
        V((3, 2 * half, 128), BF),
        V((NT[h] * 8, 128), F32),
        V((NX, NY, n, 128), BF),
        V((NY, n, 128), BF), V((NY, n, 128), BF),
        V((4, n, 128), BF), V((4, n, 128), BF), V((4, n, 128), BF), V((4, n, 128), BF),
        V((NY, n, 128), BF), V((n, 128), F32), V((NY - 1, n, 128), BF),
    ]


def local(tokens, grad_out, gate_codes, gate_scale, up_codes, up_scale, down_codes, down_scale):
    vmem = pl.BlockSpec(memory_space=pltpu.VMEM)
    hbm = pl.BlockSpec(memory_space=pl.ANY)
    V = pltpu.VMEM
    far = pl.BlockSpec(memory_space=pltpu.HBM)
    shapes = (
        jax.ShapeDtypeStruct((3, FEAT), BF),
        jax.ShapeDtypeStruct((FEAT, HID), BF),
        jax.ShapeDtypeStruct((FEAT, HID), BF),
        jax.ShapeDtypeStruct((HID, FEAT), BF),
    )
    results = pl.pallas_call(
        kernel,
        out_shape=shapes,
        in_specs=[far] * 8,
        out_specs=(vmem, hbm, hbm, hbm),
        scratch_shapes=[
            V((3, FEAT), BF), V((3, FEAT), BF),
            pltpu.SMEM((3, 8), F32), pltpu.SMEM((3, 8), F32), pltpu.SMEM((3, 8), F32),
            V((FEAT, HID), BF), V((FEAT, HID), BF), V((HID, FEAT), BF),
            V((2, TOK, FEAT), BF),
            V((FEAT, HID), BF), V((FEAT, HID), BF), V((HID, FEAT), BF),
            V((24, FEAT), F32),
            V((2, 24, 128), F32), V((2, 24, 128), F32),
            *chunk_scratch(0), *chunk_scratch(1),
            pltpu.SemaphoreType.DMA((11,)),
            pltpu.SemaphoreType.DMA((N_IDS,)),
            pltpu.SemaphoreType.DMA((N_IDS,)),
        ],
        compiler_params=pltpu.CompilerParams(
            collective_id=0, has_side_effects=True, vmem_limit_bytes=63 * 1024 * 1024
        ),
    )(tokens, grad_out, gate_codes, gate_scale.T, up_codes, up_scale.T, down_codes, down_scale)
    return pl.pallas_call(
        copies,
        out_shape=shapes,
        in_specs=[hbm] * 4,
        out_specs=(far,) * 4,
        scratch_shapes=[V(a.shape, BF) for a in shapes]
        + [pltpu.SemaphoreType.DMA((7,)), pltpu.SemaphoreType.DMA((7,))],
        compiler_params=pltpu.CompilerParams(vmem_limit_bytes=63 * 1024 * 1024),
    )(*results)


def solution(mesh):
    return jax.shard_map(
        local,
        mesh=mesh,
        in_specs=(
            P("fsdp", "tp"),
            P("fsdp", "tp"),
            P("tp", "fsdp"),
            P("tp", "fsdp"),
            P("tp", "fsdp"),
            P("tp", "fsdp"),
            P("fsdp", "tp"),
            P("fsdp", "tp"),
        ),
        out_specs=(P("fsdp", "tp"), P("tp", "fsdp"), P("tp", "fsdp"), P("fsdp", "tp")),
        check_vma=False,
    )
```

```python
import functools

import jax
import jax.numpy as jnp
from jax import lax
from jax.experimental import pallas as pl
from jax.experimental.pallas import tpu as pltpu
from jax.sharding import PartitionSpec as P

BF = jnp.bfloat16
F32 = jnp.float32
NY, NX, NZH, NZ = 8, 4, 3, 4
TOK, FEAT, HID = 288, 1024, 384
MESH = pl.DeviceIdType.MESH

NB = (1, 2)
NT = (96, 192)
FIRST = (0, 96)
SEG = (48, 80)
HALF = (192, 320)

_IDS = {}


def _id(*key):
    return _IDS.setdefault(key, len(_IDS))


for _d in (1, 2):
    _id("gz", _d)
    _id("sz", _d)
for _h in range(2):
    for _d in range(1, NY):
        _id("gy", _h, _d)
        _id("sy", _h, _d)
    for _k in ("gxr", "gxl", "gxr2", "gxl2", "gxrb", "gxlb", "x2r", "x2l", "x1r", "x1l", "xcr", "xcl"):
        _id(_k, _h)
    for _k in range(3):
        _id("core", _h, _k)
        for _d in range(1, NZ):
            _id("z", _h, _k, _d)
for _k in range(3):
    for _d in range(NZ):
        _id("back", _k, _d)
        _id("backcore", _k, _d)
N_IDS = len(_IDS)


def nt(left, right):
    return lax.dot_general(left, right, (((1,), (1,)), ((), ())), preferred_element_type=F32)


def tn(left, right):
    return lax.dot_general(left, right, (((0,), (0,)), ((), ())), preferred_element_type=F32)


def kernel(
    tok_in, gout_in, gc, gs_in, uc, us_in, dc, ds_in,
    gt, gg, gu, gd,
    tok, gout, gs, us, dsc, wg, wu, wd, X, og, ou, od, fin, ZB, RZ,
    *rest,
):
    per, (lsem, ssem, rsem) = (rest[:19], rest[19:38]), rest[38:]
    G, st, U, UB, RA, S, RB, HH, T, TB, RX1, RX2, RXa, RXb, CA, CB, YB, YF, RY = zip(*per)

    f = lax.axis_index("fsdp")
    tp = lax.axis_index("tp")
    y, zh, x = f // 12, lax.rem(f // 4, 3), lax.rem(f, 4)
    z, core = tp // 2, lax.rem(tp, 2)

    def dev(y=y, zh=zh, x=x, z=z, core=core):
        return ((y * 3 + zh) * 4 + x, z * 2 + core)

    def up(v, d, n):
        return lax.rem(v + n + d, n)

    def rcopy(key, src, dst, to):
        i = _IDS[key]
        return pltpu.make_async_remote_copy(
            src_ref=src, dst_ref=dst, send_sem=ssem.at[i], recv_sem=rsem.at[i],
            device_id=to, device_id_type=MESH,
        )

    sent = []

    def send(key, src, dst, to):
        c = rcopy(key, src, dst, to)
        c.start()
        sent.append(c)

    def gone(n):
        for c in sent[-n:]:
            c.wait_send()
        del sent[-n:]

    def recv(key, dst):
        rcopy(key, dst, dst, dev(core=1 - core)).wait_recv()

    barrier = pltpu.get_barrier_semaphore()
    partners = (
        [dev(zh=up(zh, d, 3)) for d in (1, 2)]
        + [dev(y=up(y, d, NY)) for d in (4, 3, 5, 2, 6, 1, 7)]
        + [dev(x=up(x, d, NX)) for d in (1, 3)]
        + [dev(z=up(z, d, NZ)) for d in range(1, NZ)]
        + [dev(core=1 - core)]
    )
    for p in partners:
        pl.semaphore_signal(barrier, inc=1, device_id=p, device_id_type=MESH)

    loads = [
        pltpu.make_async_copy(s, d, lsem.at[i])
        for i, (s, d) in enumerate((
            (gc, wg), (uc, wu), (dc, wd), (tok_in, tok), (gout_in, gout), (gs_in, gs), (us_in, us), (ds_in, dsc),
        ))
    ]
    for i in (3, 4, 5, 0, 6, 1, 7, 2):
        loads[i].start()

    for a, ref in ((0, tok), (1, gout)):
        loads[3 + a].wait()
        v = ref[...].astype(F32)
        for r in range(3):
            for c in range(8):
                st[0][a * 24 + r * 8 + c : a * 24 + r * 8 + c + 1, :] = v[r : r + 1, c * 128 : (c + 1) * 128]
        G[0][0, 0, 0, a] = st[0][a * 24 : (a + 1) * 24, :].astype(BF)

    pl.semaphore_wait(barrier, len(partners))

    def spread_y(h):
        for d in (4, 3, 5, 2, 6, 1, 7):
            send(("gy", h, d), G[h].at[0, 0], G[h].at[0, d], dev(y=up(y, d, NY)))

    right, left = dev(x=up(x, 1, NX)), dev(x=up(x, 3, NX))
    other = dev(core=1 - core)

    def spread_x(h):
        for d in range(1, NY):
            recv(("gy", h, d), G[h].at[0, d])
        send(("gxr", h), G[h].at[0, 0:4], G[h].at[1, 0:4], right)
        send(("gxl", h), G[h].at[0, 4:8], G[h].at[2, 4:8], left)

    def spread_x2(h):
        send(("gxrb", h), G[h].at[0, 4:8], G[h].at[1, 4:8], right)
        send(("gxlb", h), G[h].at[0, 0:4], G[h].at[2, 0:4], left)

    def forward(h):
        recv(("gxr", h), G[h].at[1, 0:4])
        send(("gxr2", h), G[h].at[1, 0:4], G[h].at[3, 0:4], right)
        recv(("gxl", h), G[h].at[2, 4:8])
        send(("gxl2", h), G[h].at[2, 4:8], G[h].at[3, 4:8], left)

    def gathered(h):
        recv(("gxrb", h), G[h].at[1, 4:8])
        recv(("gxlb", h), G[h].at[2, 0:4])
        recv(("gxr2", h), G[h].at[3, 0:4])
        recv(("gxl2", h), G[h].at[3, 4:8])

    def dequant(i, w, sc):
        loads[i].wait()
        loads[5 + i].wait()
        nr, nc = w.shape[0] // 128, w.shape[1] // 128
        for r in range(nr):
            for c in range(nc):
                t = w[r * 128 : (r + 1) * 128, c * 128 : (c + 1) * 128]
                w[r * 128 : (r + 1) * 128, c * 128 : (c + 1) * 128] = (t.astype(F32) * (sc[c, r] if i < 2 else sc[r, c])).astype(BF)

    def tokens_of(h):
        return slice(FIRST[h], FIRST[h] + NT[h])

    def unpack(h, a):
        n = 192 * NB[h]
        for slot in range(NX):
            for k in range(NB[h]):
                for d in range(NY):
                    row = slot * n + (d * NB[h] + k) * 24
                    st[h][row : row + 24, :] = G[h][slot, d, k, a].astype(F32)
        for c in range(8):
            X[a, tokens_of(h), c * 128 : (c + 1) * 128] = st[h][pl.ds(c, NT[h], stride=8), :].astype(BF)

    def put(h, k, part):
        for j in range(3):
            U[h][k, j * NT[h] : (j + 1) * NT[h], :] = part[:, j * 128 : (j + 1) * 128]

    def rows(start, n):
        return pl.ds(pl.multiple_of(start, 16), n)

    def hand(h):
        def cross(k, part):
            put(h, k, part)
            UB[h][k] = U[h][k, rows((1 - core) * HALF[h], HALF[h]), :].astype(BF)
            send(("core", h, k), UB[h].at[k], RA[h].at[k], other)

        unpack(h, 0)
        cross(0, jnp.dot(X[0, tokens_of(h), :], wg[...], preferred_element_type=F32))
        cross(1, jnp.dot(X[0, tokens_of(h), :], wu[...], preferred_element_type=F32))
        unpack(h, 1)
        cross(2, nt(X[1, tokens_of(h), :], wd[...]))

    def chip_sum(h):
        for k in range(3):
            recv(("core", h, k), RA[h].at[k])
            S[h][k] = (U[h][k, rows(core * HALF[h], HALF[h]), :] + RA[h][k].astype(F32)).astype(BF)
            for d in (2, 1, 3):
                zz = up(z, d, NZ)
                send(("z", h, k, d), S[h].at[k, rows(zz * SEG[h], SEG[h])], RB[h].at[d - 1, k], dev(z=zz))

    def share(h, zz, cc):
        return rows(cc * HALF[h] + zz * SEG[h], SEG[h])

    def middle(h):
        def total(k):
            t = U[h][k, share(h, z, core), :] + RA[h][k, rows(z * SEG[h], SEG[h]), :].astype(F32)
            for d in range(1, NZ):
                recv(("z", h, k, d), RB[h].at[d - 1, k])
                t = t + RB[h][d - 1, k].astype(F32)
            return t

        gate, up_value, grad_hidden = total(0), total(1), total(2)
        sig = jax.nn.sigmoid(gate)
        act = gate * sig
        at = share(h, z, core)
        HH[h][0, at, :] = (grad_hidden * up_value * sig * (1.0 + gate * (1.0 - sig))).astype(BF)
        HH[h][1, at, :] = (grad_hidden * act).astype(BF)
        HH[h][2, at, :] = (act * up_value).astype(BF)

    groups = ((0, 0, 3), (1, 0, 2), (1, 2, 1))

    def piece(g, zz, cc):
        h, lo, n = groups[g]
        return HH[h].at[pl.ds(lo, n), share(h, zz, cc)]

    def give(g):
        seg = piece(g, z, core)
        for d in (2, 1, 3):
            send(("back", g, d), seg, seg, dev(z=up(z, d, NZ)))
        send(("backcore", g, 0), seg, seg, other)

    def spread(g):
        for d in (1, 3, 2):
            seg = piece(g, up(z, -d, NZ), core)
            recv(("back", g, d), seg)
            send(("backcore", g, d), seg, seg, other)

    def collect(g):
        for d in range(NZ):
            recv(("backcore", g, d), piece(g, up(z, -d, NZ), 1 - core))

    def whole(h, k):
        return jnp.concatenate([HH[h][k, j * NT[h] : (j + 1) * NT[h], :] for j in range(3)], axis=1)

    def input_grad(h, half):
        r, start = slice(half * NT[h] // 2, (half + 1) * NT[h] // 2), half * NT[h] * 4
        ggp, gup = whole(h, 0)[r], whole(h, 1)[r]
        for n in range(4):
            w = slice(n * 256, (n + 1) * 256)
            part = nt(ggp, wg[w, :]) + nt(gup, wu[w, :])
            for q in range(2):
                T[h][pl.ds(start + n * 2 + q, NT[h] // 2, stride=8), :] = part[:, q * 128 : (q + 1) * 128]

    def slab(h, p, lo, hi):
        n = 24 * NB[h]
        return T[h][(p * 8 + lo) * n : (p * 8 + hi) * n, :].reshape(hi - lo, n, 128)

    def sum_x(h):
        input_grad(h, 1)
        TB[h][3] = slab(h, 3, 0, 8).astype(BF)
        send(("x2r", h), TB[h].at[3, 0:4], RXa[h], right)
        send(("x2l", h), TB[h].at[3, 4:8], RXb[h], left)
        input_grad(h, 0)
        TB[h][2, 4:8] = slab(h, 2, 4, 8).astype(BF)
        TB[h][1, 0:4] = slab(h, 1, 0, 4).astype(BF)
        gone(2)
        send(("x1r", h), TB[h].at[2, 4:8], RX1[h].at[4:8], right)
        send(("x1l", h), TB[h].at[1, 0:4], RX2[h].at[0:4], left)

    def sum_x2(h):
        recv(("x2r", h), RXa[h])
        CA[h][...] = (slab(h, 2, 0, 4) + RXa[h][...].astype(F32)).astype(BF)
        send(("xcr", h), CA[h], RX1[h].at[0:4], right)
        recv(("x2l", h), RXb[h])
        CB[h][...] = (slab(h, 1, 4, 8) + RXb[h][...].astype(F32)).astype(BF)
        send(("xcl", h), CB[h], RX2[h].at[4:8], left)

    def sum_y(h):
        recv(("x1r", h), RX1[h].at[4:8])
        recv(("x1l", h), RX2[h].at[0:4])
        recv(("xcr", h), RX1[h].at[0:4])
        recv(("xcl", h), RX2[h].at[4:8])
        n = 24 * NB[h]
        for d in (4, 3, 5, 2, 6, 1, 7, 0):
            v = T[h][d * n : (d + 1) * n, :] + RX1[h][d].astype(F32) + RX2[h][d].astype(F32)
            if d:
                YB[h][d] = v.astype(BF)
                send(("sy", h, d), YB[h].at[d], RY[h].at[d - 1], dev(y=up(y, -d, NY)))
            else:
                YF[h][...] = v

    def summed_y(h):
        v = YF[h][...]
        for d in (1, 7, 2, 6, 3, 5, 4):
            recv(("sy", h, d), RY[h].at[d - 1])
            v = v + RY[h][d - 1].astype(F32)
        return v

    stores = []

    def store(src, dst):
        c = pltpu.make_async_copy(src, dst, lsem.at[8 + len(stores)])
        c.start()
        stores.append(c)

    for d in (1, 2):
        send(("gz", d), G[0].at[0, 0, 0], G[1].at[0, 0, d - 1], dev(zh=up(zh, d, 3)))
    spread_y(0)
    for h in range(2):
        for k in range(3):
            U[h][k, 3 * NT[h] :, :] = jnp.zeros((2 * HALF[h] - 3 * NT[h], 128), F32)
    dequant(0, wg, gs)
    dequant(1, wu, us)
    dequant(2, wd, dsc)
    for d in (1, 2):
        recv(("gz", d), G[1].at[0, 0, d - 1])
    spread_y(1)
    spread_x(0)
    spread_x2(0)
    forward(0)
    spread_x(1)
    gathered(0)
    hand(0)
    spread_x2(1)
    chip_sum(0)
    forward(1)
    middle(0)
    give(0)
    gathered(1)
    hand(1)
    spread(0)
    chip_sum(1)
    collect(0)
    sum_x(0)
    sum_x2(0)
    middle(1)
    give(1)
    sum_y(0)
    spread(1)
    give(2)
    collect(1)
    sum_x(1)
    own_sum = summed_y(0)
    fin[0:24, 0:128] = own_sum
    sum_x2(1)
    spread(2)

    both = jnp.concatenate(
        [jnp.concatenate([whole(h, 0), whole(h, 1)], axis=1) for h in range(2)], axis=0
    )

    def weight_grads(n):
        r = slice(n * 256, (n + 1) * 256)
        part = tn(X[0, :, r], both)
        og[r, :] = part[:, :HID].astype(BF)
        ou[r, :] = part[:, HID:].astype(BF)

    weight_grads(0)
    weight_grads(1)
    sum_y(1)
    weight_grads(2)
    weight_grads(3)
    store(og, gg)
    store(ou, gu)
    collect(2)
    hid = jnp.concatenate([whole(0, 2), whole(1, 2)], axis=0)
    for n in range(3):
        r = slice(n * 128, (n + 1) * 128)
        od[r, :] = tn(hid[:, r], X[1]).astype(BF)
    store(od, gd)

    v = summed_y(1)
    for i in range(2):
        ZB[i] = v[i * 24 : (i + 1) * 24, :].astype(BF)
    for d in (1, 2):
        send(("sz", d), ZB.at[d - 1], RZ.at[d - 1], dev(zh=up(zh, -d, 3)))
    v = fin[0:24, 0:128]
    for d in (1, 2):
        recv(("sz", d), RZ.at[d - 1])
        v = v + RZ[d - 1].astype(F32)
    for r in range(3):
        for c in range(8):
            fin[r : r + 1, c * 128 : (c + 1) * 128] = v[r * 8 + c : r * 8 + c + 1, :]
    gt[...] = fin[0:3, :].astype(BF)

    for c in stores:
        c.wait()
    for c in sent:
        c.wait_send()


def copies(*refs):
    ins, outs, bufs, isem, osem = refs[:4], refs[4:8], refs[8:12], refs[12], refs[13]
    parts = []
    for i in range(4):
        rows = ins[i].shape[0]
        n = 2 if i else 1
        parts += [(i, slice(j * rows // n, (j + 1) * rows // n)) for j in range(n)]
    loads = [pltpu.make_async_copy(ins[i].at[r], bufs[i].at[r], isem.at[k]) for k, (i, r) in enumerate(parts)]
    stores = [pltpu.make_async_copy(bufs[i].at[r], outs[i].at[r], osem.at[k]) for k, (i, r) in enumerate(parts)]
    for c in loads:
        c.start()
    for k, c in enumerate(loads):
        c.wait()
        stores[k].start()
    for c in stores:
        c.wait()


def chunk_scratch(h):
    V = pltpu.VMEM
    n, half, seg = 24 * NB[h], HALF[h], SEG[h]
    return [
        V((NX, NY, NB[h], 2, 24, 128), BF),
        V((NT[h] * 8, 128), F32),
        V((3, 2 * half, 128), F32),
        V((3, half, 128), BF), V((3, half, 128), BF), V((3, half, 128), BF),
        V((NZ - 1, 3, seg, 128), BF),
        V((3, 2 * half, 128), BF),
        V((NT[h] * 8, 128), F32),
        V((NX, NY, n, 128), BF),
        V((NY, n, 128), BF), V((NY, n, 128), BF),
        V((4, n, 128), BF), V((4, n, 128), BF), V((4, n, 128), BF), V((4, n, 128), BF),
        V((NY, n, 128), BF), V((n, 128), F32), V((NY - 1, n, 128), BF),
    ]


def local(tokens, grad_out, gate_codes, gate_scale, up_codes, up_scale, down_codes, down_scale):
    vmem = pl.BlockSpec(memory_space=pltpu.VMEM)
    hbm = pl.BlockSpec(memory_space=pl.ANY)
    V = pltpu.VMEM
    far = pl.BlockSpec(memory_space=pltpu.HBM)
    shapes = (
        jax.ShapeDtypeStruct((3, FEAT), BF),
        jax.ShapeDtypeStruct((FEAT, HID), BF),
        jax.ShapeDtypeStruct((FEAT, HID), BF),
        jax.ShapeDtypeStruct((HID, FEAT), BF),
    )
    results = pl.pallas_call(
        kernel,
        out_shape=shapes,
        in_specs=[far] * 8,
        out_specs=(vmem, hbm, hbm, hbm),
        scratch_shapes=[
            V((3, FEAT), BF), V((3, FEAT), BF),
            pltpu.SMEM((3, 8), F32), pltpu.SMEM((3, 8), F32), pltpu.SMEM((3, 8), F32),
            V((FEAT, HID), BF), V((FEAT, HID), BF), V((HID, FEAT), BF),
            V((2, TOK, FEAT), BF),
            V((FEAT, HID), BF), V((FEAT, HID), BF), V((HID, FEAT), BF),
            V((24, FEAT), F32),
            V((2, 24, 128), BF), V((2, 24, 128), BF),
            *chunk_scratch(0), *chunk_scratch(1),
            pltpu.SemaphoreType.DMA((11,)),
            pltpu.SemaphoreType.DMA((N_IDS,)),
            pltpu.SemaphoreType.DMA((N_IDS,)),
        ],
        compiler_params=pltpu.CompilerParams(
            collective_id=0, has_side_effects=True, vmem_limit_bytes=63 * 1024 * 1024
        ),
    )(tokens, grad_out, gate_codes, gate_scale.T, up_codes, up_scale.T, down_codes, down_scale)
    return pl.pallas_call(
        copies,
        out_shape=shapes,
        in_specs=[hbm] * 4,
        out_specs=(far,) * 4,
        scratch_shapes=[V(a.shape, BF) for a in shapes]
        + [pltpu.SemaphoreType.DMA((7,)), pltpu.SemaphoreType.DMA((7,))],
        compiler_params=pltpu.CompilerParams(vmem_limit_bytes=63 * 1024 * 1024),
    )(*results)


def solution(mesh):
    return jax.shard_map(
        local,
        mesh=mesh,
        in_specs=(
            P("fsdp", "tp"),
            P("fsdp", "tp"),
            P("tp", "fsdp"),
            P("tp", "fsdp"),
            P("tp", "fsdp"),
            P("tp", "fsdp"),
            P("fsdp", "tp"),
            P("fsdp", "tp"),
        ),
        out_specs=(P("fsdp", "tp"), P("tp", "fsdp"), P("tp", "fsdp"), P("fsdp", "tp")),
        check_vma=False,
    )
```

```python
import functools

import jax
import jax.numpy as jnp
from jax import lax
from jax.experimental import pallas as pl
from jax.experimental.pallas import tpu as pltpu
from jax.sharding import PartitionSpec as P

BF = jnp.bfloat16
F32 = jnp.float32
NY, NX, NZH, NZ = 8, 4, 3, 4
TOK, FEAT, HID = 288, 1024, 384
MESH = pl.DeviceIdType.MESH

NB = (1, 2)
NT = (96, 192)
FIRST = (0, 96)
SEG = (48, 80)
HALF = (192, 320)

_IDS = {}


def _id(*key):
    return _IDS.setdefault(key, len(_IDS))


for _d in (1, 2):
    _id("gz", _d)
    _id("sz", _d)
for _h in range(2):
    for _d in range(1, NY):
        _id("gy", _h, _d)
        _id("sy", _h, _d)
    for _k in ("gxr", "gxl", "gxr2", "gxl2", "gxrb", "gxlb", "x2r", "x2l", "x1r", "x1l", "xcr", "xcl"):
        _id(_k, _h)
    for _k in range(3):
        _id("core", _h, _k)
        for _d in range(1, NZ):
            _id("z", _h, _k, _d)
for _k in range(4):
    for _d in range(NZ):
        _id("back", _k, _d)
        _id("backcore", _k, _d)
N_IDS = len(_IDS)


def nt(left, right):
    return lax.dot_general(left, right, (((1,), (1,)), ((), ())), preferred_element_type=F32)


def tn(left, right):
    return lax.dot_general(left, right, (((0,), (0,)), ((), ())), preferred_element_type=F32)


def kernel(
    tok_in, gout_in, gc, gs_in, uc, us_in, dc, ds_in,
    gt, gg, gu, gd,
    tok, gout, gs, us, dsc, wg, wu, wd, X, og, ou, od, fin, ZB, RZ,
    *rest,
):
    per, (lsem, ssem, rsem) = (rest[:19], rest[19:38]), rest[38:]
    G, st, U, UB, RA, S, RB, HH, T, TB, RX1, RX2, RXa, RXb, CA, CB, YB, YF, RY = zip(*per)

    f = lax.axis_index("fsdp")
    tp = lax.axis_index("tp")
    y, zh, x = f // 12, lax.rem(f // 4, 3), lax.rem(f, 4)
    z, core = tp // 2, lax.rem(tp, 2)

    def dev(y=y, zh=zh, x=x, z=z, core=core):
        return ((y * 3 + zh) * 4 + x, z * 2 + core)

    def up(v, d, n):
        return lax.rem(v + n + d, n)

    def rcopy(key, src, dst, to):
        i = _IDS[key]
        return pltpu.make_async_remote_copy(
            src_ref=src, dst_ref=dst, send_sem=ssem.at[i], recv_sem=rsem.at[i],
            device_id=to, device_id_type=MESH,
        )

    sent = []

    def send(key, src, dst, to):
        c = rcopy(key, src, dst, to)
        c.start()
        sent.append(c)

    def gone(n):
        for c in sent[-n:]:
            c.wait_send()
        del sent[-n:]

    def recv(key, dst):
        rcopy(key, dst, dst, dev(core=1 - core)).wait_recv()

    barrier = pltpu.get_barrier_semaphore()
    partners = (
        [dev(zh=up(zh, d, 3)) for d in (1, 2)]
        + [dev(y=up(y, d, NY)) for d in (4, 3, 5, 2, 6, 1, 7)]
        + [dev(x=up(x, d, NX)) for d in (1, 3)]
        + [dev(z=up(z, d, NZ)) for d in range(1, NZ)]
        + [dev(core=1 - core)]
    )
    for p in partners:
        pl.semaphore_signal(barrier, inc=1, device_id=p, device_id_type=MESH)

    loads = [
        pltpu.make_async_copy(s, d, lsem.at[i])
        for i, (s, d) in enumerate((
            (gc, wg), (uc, wu), (dc, wd), (tok_in, tok), (gout_in, gout), (gs_in, gs), (us_in, us), (ds_in, dsc),
        ))
    ]
    for i in (3, 4, 5, 0, 6, 1, 7, 2):
        loads[i].start()

    for a, ref in ((0, tok), (1, gout)):
        loads[3 + a].wait()
        v = ref[...].astype(F32)
        for r in range(3):
            for c in range(8):
                st[0][a * 24 + r * 8 + c : a * 24 + r * 8 + c + 1, :] = v[r : r + 1, c * 128 : (c + 1) * 128]
        G[0][0, 0, 0, a] = st[0][a * 24 : (a + 1) * 24, :].astype(BF)

    pl.semaphore_wait(barrier, len(partners))

    def spread_y(h):
        for d in (4, 3, 5, 2, 6, 1, 7):
            send(("gy", h, d), G[h].at[0, 0], G[h].at[0, d], dev(y=up(y, d, NY)))

    right, left = dev(x=up(x, 1, NX)), dev(x=up(x, 3, NX))
    other = dev(core=1 - core)

    def spread_x(h):
        for d in range(1, NY):
            recv(("gy", h, d), G[h].at[0, d])
        send(("gxr", h), G[h].at[0, 0:4], G[h].at[1, 0:4], right)
        send(("gxl", h), G[h].at[0, 4:8], G[h].at[2, 4:8], left)

    def spread_x2(h):
        send(("gxrb", h), G[h].at[0, 4:8], G[h].at[1, 4:8], right)
        send(("gxlb", h), G[h].at[0, 0:4], G[h].at[2, 0:4], left)

    def forward(h):
        recv(("gxr", h), G[h].at[1, 0:4])
        send(("gxr2", h), G[h].at[1, 0:4], G[h].at[3, 0:4], right)
        recv(("gxl", h), G[h].at[2, 4:8])
        send(("gxl2", h), G[h].at[2, 4:8], G[h].at[3, 4:8], left)

    def gathered(h):
        recv(("gxrb", h), G[h].at[1, 4:8])
        recv(("gxlb", h), G[h].at[2, 0:4])
        recv(("gxr2", h), G[h].at[3, 0:4])
        recv(("gxl2", h), G[h].at[3, 4:8])

    def dequant(i, w, sc):
        loads[i].wait()
        loads[5 + i].wait()
        nr, nc = w.shape[0] // 128, w.shape[1] // 128
        for r in range(nr):
            for c in range(nc):
                t = w[r * 128 : (r + 1) * 128, c * 128 : (c + 1) * 128]
                w[r * 128 : (r + 1) * 128, c * 128 : (c + 1) * 128] = (t.astype(F32) * (sc[c, r] if i < 2 else sc[r, c])).astype(BF)

    def tokens_of(h):
        return slice(FIRST[h], FIRST[h] + NT[h])

    def unpack(h, a):
        n = 192 * NB[h]
        for slot in range(NX):
            for k in range(NB[h]):
                for d in range(NY):
                    row = slot * n + (d * NB[h] + k) * 24
                    st[h][row : row + 24, :] = G[h][slot, d, k, a].astype(F32)
        for c in range(8):
            X[a, tokens_of(h), c * 128 : (c + 1) * 128] = st[h][pl.ds(c, NT[h], stride=8), :].astype(BF)

    def put(h, k, part):
        for j in range(3):
            U[h][k, j * NT[h] : (j + 1) * NT[h], :] = part[:, j * 128 : (j + 1) * 128]

    def rows(start, n):
        return pl.ds(pl.multiple_of(start, 16), n)

    def hand(h):
        def cross(k, part):
            put(h, k, part)
            UB[h][k] = U[h][k, rows((1 - core) * HALF[h], HALF[h]), :].astype(BF)
            send(("core", h, k), UB[h].at[k], RA[h].at[k], other)

        unpack(h, 0)
        cross(0, jnp.dot(X[0, tokens_of(h), :], wg[...], preferred_element_type=F32))
        cross(1, jnp.dot(X[0, tokens_of(h), :], wu[...], preferred_element_type=F32))
        unpack(h, 1)
        cross(2, nt(X[1, tokens_of(h), :], wd[...]))

    def chip_sum(h):
        for k in range(3):
            recv(("core", h, k), RA[h].at[k])
            S[h][k] = (U[h][k, rows(core * HALF[h], HALF[h]), :] + RA[h][k].astype(F32)).astype(BF)
            for d in (2, 1, 3):
                zz = up(z, d, NZ)
                send(("z", h, k, d), S[h].at[k, rows(zz * SEG[h], SEG[h])], RB[h].at[d - 1, k], dev(z=zz))

    def share(h, zz, cc):
        return rows(cc * HALF[h] + zz * SEG[h], SEG[h])

    def middle(h):
        def total(k):
            t = U[h][k, share(h, z, core), :] + RA[h][k, rows(z * SEG[h], SEG[h]), :].astype(F32)
            for d in range(1, NZ):
                recv(("z", h, k, d), RB[h].at[d - 1, k])
                t = t + RB[h][d - 1, k].astype(F32)
            return t

        gate, up_value, grad_hidden = total(0), total(1), total(2)
        sig = jax.nn.sigmoid(gate)
        act = gate * sig
        at = share(h, z, core)
        HH[h][0, at, :] = (grad_hidden * up_value * sig * (1.0 + gate * (1.0 - sig))).astype(BF)
        HH[h][1, at, :] = (grad_hidden * act).astype(BF)
        HH[h][2, at, :] = (act * up_value).astype(BF)

    groups = ((0, 0, 3), (1, 0, 1), (1, 1, 1), (1, 2, 1))

    def piece(g, zz, cc):
        h, lo, n = groups[g]
        return HH[h].at[pl.ds(lo, n), share(h, zz, cc)]

    def give(g):
        seg = piece(g, z, core)
        for d in (2, 1, 3):
            send(("back", g, d), seg, seg, dev(z=up(z, d, NZ)))
        send(("backcore", g, 0), seg, seg, other)

    def spread(g):
        for d in (1, 3, 2):
            seg = piece(g, up(z, -d, NZ), core)
            recv(("back", g, d), seg)
            send(("backcore", g, d), seg, seg, other)

    def collect(g):
        for d in range(NZ):
            recv(("backcore", g, d), piece(g, up(z, -d, NZ), 1 - core))

    def whole(h, k):
        return jnp.concatenate([HH[h][k, j * NT[h] : (j + 1) * NT[h], :] for j in range(3)], axis=1)

    def input_grad(h, half):
        r, start = slice(half * NT[h] // 2, (half + 1) * NT[h] // 2), half * NT[h] * 4
        ggp, gup = whole(h, 0)[r], whole(h, 1)[r]
        for n in range(4):
            w = slice(n * 256, (n + 1) * 256)
            part = nt(ggp, wg[w, :]) + nt(gup, wu[w, :])
            for q in range(2):
                T[h][pl.ds(start + n * 2 + q, NT[h] // 2, stride=8), :] = part[:, q * 128 : (q + 1) * 128]

    def slab(h, p, lo, hi):
        n = 24 * NB[h]
        return T[h][(p * 8 + lo) * n : (p * 8 + hi) * n, :].reshape(hi - lo, n, 128)

    def sum_x(h):
        input_grad(h, 1)
        TB[h][3] = slab(h, 3, 0, 8).astype(BF)
        send(("x2r", h), TB[h].at[3, 0:4], RXa[h], right)
        send(("x2l", h), TB[h].at[3, 4:8], RXb[h], left)
        input_grad(h, 0)
        TB[h][2, 4:8] = slab(h, 2, 4, 8).astype(BF)
        TB[h][1, 0:4] = slab(h, 1, 0, 4).astype(BF)
        gone(2)
        send(("x1r", h), TB[h].at[2, 4:8], RX1[h].at[4:8], right)
        send(("x1l", h), TB[h].at[1, 0:4], RX2[h].at[0:4], left)

    def sum_x2(h):
        recv(("x2r", h), RXa[h])
        CA[h][...] = (slab(h, 2, 0, 4) + RXa[h][...].astype(F32)).astype(BF)
        send(("xcr", h), CA[h], RX1[h].at[0:4], right)
        recv(("x2l", h), RXb[h])
        CB[h][...] = (slab(h, 1, 4, 8) + RXb[h][...].astype(F32)).astype(BF)
        send(("xcl", h), CB[h], RX2[h].at[4:8], left)

    def sum_y(h):
        recv(("x1r", h), RX1[h].at[4:8])
        recv(("x1l", h), RX2[h].at[0:4])
        recv(("xcr", h), RX1[h].at[0:4])
        recv(("xcl", h), RX2[h].at[4:8])
        n = 24 * NB[h]
        for d in (4, 3, 5, 2, 6, 1, 7, 0):
            v = T[h][d * n : (d + 1) * n, :] + RX1[h][d].astype(F32) + RX2[h][d].astype(F32)
            if d:
                YB[h][d] = v.astype(BF)
                send(("sy", h, d), YB[h].at[d], RY[h].at[d - 1], dev(y=up(y, -d, NY)))
            else:
                YF[h][...] = v

    def summed_y(h):
        v = YF[h][...]
        for d in (1, 7, 2, 6, 3, 5, 4):
            recv(("sy", h, d), RY[h].at[d - 1])
            v = v + RY[h][d - 1].astype(F32)
        return v

    stores = []

    def store(src, dst):
        c = pltpu.make_async_copy(src, dst, lsem.at[8 + len(stores)])
        c.start()
        stores.append(c)

    for d in (1, 2):
        send(("gz", d), G[0].at[0, 0, 0], G[1].at[0, 0, d - 1], dev(zh=up(zh, d, 3)))
    spread_y(0)
    for h in range(2):
        for k in range(3):
            U[h][k, 3 * NT[h] :, :] = jnp.zeros((2 * HALF[h] - 3 * NT[h], 128), F32)
    dequant(0, wg, gs)
    dequant(1, wu, us)
    dequant(2, wd, dsc)
    for d in (1, 2):
        recv(("gz", d), G[1].at[0, 0, d - 1])
    spread_y(1)
    spread_x(0)
    spread_x2(0)
    forward(0)
    spread_x(1)
    gathered(0)
    hand(0)
    spread_x2(1)
    chip_sum(0)
    forward(1)
    middle(0)
    give(0)
    gathered(1)
    hand(1)
    spread(0)
    chip_sum(1)
    collect(0)
    sum_x(0)
    sum_x2(0)
    middle(1)
    give(1)
    give(2)
    sum_y(0)
    spread(1)
    spread(2)
    give(3)
    collect(1)
    collect(2)
    sum_x(1)
    own_sum = summed_y(0)
    fin[0:24, 0:128] = own_sum
    sum_x2(1)
    spread(3)

    both = jnp.concatenate(
        [jnp.concatenate([whole(h, 0), whole(h, 1)], axis=1) for h in range(2)], axis=0
    )

    def weight_grads(n):
        r = slice(n * 256, (n + 1) * 256)
        part = tn(X[0, :, r], both)
        og[r, :] = part[:, :HID].astype(BF)
        ou[r, :] = part[:, HID:].astype(BF)

    weight_grads(0)
    weight_grads(1)
    sum_y(1)
    weight_grads(2)
    weight_grads(3)
    store(og, gg)
    store(ou, gu)
    collect(3)
    hid = jnp.concatenate([whole(0, 2), whole(1, 2)], axis=0)
    for n in range(3):
        r = slice(n * 128, (n + 1) * 128)
        od[r, :] = tn(hid[:, r], X[1]).astype(BF)
    store(od, gd)

    v = summed_y(1)
    for i in range(2):
        ZB[i] = v[i * 24 : (i + 1) * 24, :].astype(BF)
    for d in (1, 2):
        send(("sz", d), ZB.at[d - 1], RZ.at[d - 1], dev(zh=up(zh, -d, 3)))
    v = fin[0:24, 0:128]
    for d in (1, 2):
        recv(("sz", d), RZ.at[d - 1])
        v = v + RZ[d - 1].astype(F32)
    for r in range(3):
        for c in range(8):
            fin[r : r + 1, c * 128 : (c + 1) * 128] = v[r * 8 + c : r * 8 + c + 1, :]
    gt[...] = fin[0:3, :].astype(BF)

    for c in stores:
        c.wait()
    for c in sent:
        c.wait_send()


def copies(*refs):
    ins, outs, bufs, isem, osem = refs[:4], refs[4:8], refs[8:12], refs[12], refs[13]
    parts = []
    for i in range(4):
        rows = ins[i].shape[0]
        n = 2 if i else 1
        parts += [(i, slice(j * rows // n, (j + 1) * rows // n)) for j in range(n)]
    loads = [pltpu.make_async_copy(ins[i].at[r], bufs[i].at[r], isem.at[k]) for k, (i, r) in enumerate(parts)]
    stores = [pltpu.make_async_copy(bufs[i].at[r], outs[i].at[r], osem.at[k]) for k, (i, r) in enumerate(parts)]
    for c in loads:
        c.start()
    for k, c in enumerate(loads):
        c.wait()
        stores[k].start()
    for c in stores:
        c.wait()


def chunk_scratch(h):
    V = pltpu.VMEM
    n, half, seg = 24 * NB[h], HALF[h], SEG[h]
    return [
        V((NX, NY, NB[h], 2, 24, 128), BF),
        V((NT[h] * 8, 128), F32),
        V((3, 2 * half, 128), F32),
        V((3, half, 128), BF), V((3, half, 128), BF), V((3, half, 128), BF),
        V((NZ - 1, 3, seg, 128), BF),
        V((3, 2 * half, 128), BF),
        V((NT[h] * 8, 128), F32),
        V((NX, NY, n, 128), BF),
        V((NY, n, 128), BF), V((NY, n, 128), BF),
        V((4, n, 128), BF), V((4, n, 128), BF), V((4, n, 128), BF), V((4, n, 128), BF),
        V((NY, n, 128), BF), V((n, 128), F32), V((NY - 1, n, 128), BF),
    ]


def local(tokens, grad_out, gate_codes, gate_scale, up_codes, up_scale, down_codes, down_scale):
    vmem = pl.BlockSpec(memory_space=pltpu.VMEM)
    hbm = pl.BlockSpec(memory_space=pl.ANY)
    V = pltpu.VMEM
    far = pl.BlockSpec(memory_space=pltpu.HBM)
    shapes = (
        jax.ShapeDtypeStruct((3, FEAT), BF),
        jax.ShapeDtypeStruct((FEAT, HID), BF),
        jax.ShapeDtypeStruct((FEAT, HID), BF),
        jax.ShapeDtypeStruct((HID, FEAT), BF),
    )
    results = pl.pallas_call(
        kernel,
        out_shape=shapes,
        in_specs=[far] * 8,
        out_specs=(vmem, hbm, hbm, hbm),
        scratch_shapes=[
            V((3, FEAT), BF), V((3, FEAT), BF),
            pltpu.SMEM((3, 8), F32), pltpu.SMEM((3, 8), F32), pltpu.SMEM((3, 8), F32),
            V((FEAT, HID), BF), V((FEAT, HID), BF), V((HID, FEAT), BF),
            V((2, TOK, FEAT), BF),
            V((FEAT, HID), BF), V((FEAT, HID), BF), V((HID, FEAT), BF),
            V((24, FEAT), F32),
            V((2, 24, 128), BF), V((2, 24, 128), BF),
            *chunk_scratch(0), *chunk_scratch(1),
            pltpu.SemaphoreType.DMA((11,)),
            pltpu.SemaphoreType.DMA((N_IDS,)),
            pltpu.SemaphoreType.DMA((N_IDS,)),
        ],
        compiler_params=pltpu.CompilerParams(
            collective_id=0, has_side_effects=True, vmem_limit_bytes=63 * 1024 * 1024
        ),
    )(tokens, grad_out, gate_codes, gate_scale.T, up_codes, up_scale.T, down_codes, down_scale)
    return pl.pallas_call(
        copies,
        out_shape=shapes,
        in_specs=[hbm] * 4,
        out_specs=(far,) * 4,
        scratch_shapes=[V(a.shape, BF) for a in shapes]
        + [pltpu.SemaphoreType.DMA((7,)), pltpu.SemaphoreType.DMA((7,))],
        compiler_params=pltpu.CompilerParams(vmem_limit_bytes=63 * 1024 * 1024),
    )(*results)


def solution(mesh):
    return jax.shard_map(
        local,
        mesh=mesh,
        in_specs=(
            P("fsdp", "tp"),
            P("fsdp", "tp"),
            P("tp", "fsdp"),
            P("tp", "fsdp"),
            P("tp", "fsdp"),
            P("tp", "fsdp"),
            P("fsdp", "tp"),
            P("fsdp", "tp"),
        ),
        out_specs=(P("fsdp", "tp"), P("tp", "fsdp"), P("tp", "fsdp"), P("fsdp", "tp")),
        check_vma=False,
    )
```
